256 devices in a mesh: grp: 4 (over x), cp: 64 (over y, z, core).
Axes of the slice: x: 4, y: 4, z: 8, core: 2. Of those that a mesh axis runs over, the one named last changes fastest.
Arguments:
- queries: bfloat16 [32768, 3072], P(('grp', 'cp')), may hold values from -27 to 27
- keys: bfloat16 [32768, 3072], P(('grp', 'cp')), may hold values from -27 to 27
- values: bfloat16 [32768, 3072], P(('grp', 'cp')), may hold values from -6 to 6
- segment_ids: int32 [32768], P(('grp', 'cp')), may hold values from 0 to 169, never falling along the last dimension, each value on 1 to 384 neighbouring positions
Outputs:
- attended: bfloat16 [32768, 3072], P(('grp', 'cp'))
- log_sum: float32 [24, 32768], P(None, ('grp', 'cp'))
The draws below stay inside these ranges and needn't reach their ends.
Inputs may be any that keep to these rules, and one draw needn't show every extreme that they name: `segment_ids`: segment ids never fall along the tokens; each segment holds 1 to 384 tokens and one holds exactly 384.
All inputs are finite; a program needn't handle non-finite values.
Results may differ from the reference program's by a relative error of at most 0.009.
Values may be sent and summed in bfloat16 or wider, within the bound.
A program may use at most 64 MiB of HBM per device.

```python
import math
import jax
import jax.numpy as jnp
import numpy as np
from jax import lax

H = 24
HD = 128
TOK_DEV = 128
FRAME = 128
REACH = 4
TOKENS = 32768
SEG_MOST = 384
SEG_COUNT = 170


def draw_queries(key, part):
    key = jax.random.fold_in(key, 1)
    own = jnp.clip(jax.random.normal(key, (TOKENS, H * HD), jnp.float32), -6.0, 6.0)
    return own.astype(jnp.bfloat16)


def draw_keys(key, part):
    key = jax.random.fold_in(key, 2)
    own = jnp.clip(jax.random.normal(key, (TOKENS, H * HD), jnp.float32), -6.0, 6.0)
    return own.astype(jnp.bfloat16)


def shard_levels(key, extent, cuts, least, largest):
    def one(axis_at, parts):
        heights = jax.random.uniform(jax.random.fold_in(jax.random.fold_in(key, 6), axis_at), (parts,), jnp.float32, least / len(cuts), largest / len(cuts))
        return jnp.repeat(jnp.exp(heights), extent[axis_at] // parts).reshape((-1,) + (1,) * (len(extent) - axis_at - 1))

    factor_of = one(*cuts[0])
    for cut in cuts[1:]:
        factor_of = factor_of * one(*cut)
    return factor_of


def profile(number_of, total, most, slope):
    weights = [(1 << 20) // math.isqrt(grade ** slope) + 1 for grade in range(2, number_of + 1)]
    surplus, counts = total - most - (number_of - 1), [1] * (number_of - 1)
    while surplus > 0:
        free = [i for i in range(number_of - 1) if counts[i] < most]
        pool, remaining = sum([weights[i] for i in free]), surplus
        for i in free:
            extra = min(most - counts[i], max(1, remaining * weights[i] // pool), surplus)
            counts[i] = counts[i] + extra
            surplus = surplus - extra
    return np.array([most] + counts)


def ragged_sizes(stream_key, amount, total, limit, skew):
    if amount == 2:
        one = jax.random.randint(stream_key, (), max(1, total - limit), min(limit, total - 1) + 1)
        return jnp.stack([one, total - one])
    tallies = jnp.asarray(profile(amount, total, limit, skew), jnp.int32)
    couples = (amount - 1) // 2
    giver, sink = tallies[1:1 + 2 * couples:2], tallies[2:2 + 2 * couples:2]
    room = jnp.minimum(giver - 1, limit - sink)
    passed = jax.random.randint(jax.random.fold_in(stream_key, 1), (couples,), 0, 1 << 20) % (room + 1)
    tallies = tallies.at[1:1 + 2 * couples:2].set(giver - passed).at[2:2 + 2 * couples:2].set(sink + passed)
    return tallies[jax.random.permutation(jax.random.fold_in(stream_key, 2), amount)]


def normal_values(rng, dims, spread, most, cuts=(), kind=jnp.bfloat16):
    drawn = jax.random.normal(rng, dims, jnp.float32) * spread
    if len(cuts) > 0:
        drawn = shard_levels(rng, dims, cuts, -0.22, 0.18) * drawn
    return jnp.clip(drawn, min=-most, max=most).astype(kind)


def setup_inputs(seed: int = 0) -> dict:
    key_of = jax.random.split(jax.random.key(seed), 5)
    return {
        "queries": draw_queries(jax.random.fold_in(key_of[4], 71), 0),
        "keys": draw_keys(jax.random.fold_in(key_of[4], 71), 0),
        "values": normal_values(key_of[2], (TOKENS, H * HD), 1.0, 6.0, ((0, 256),)),
        "segment_ids": jnp.searchsorted(jnp.cumsum(ragged_sizes(key_of[3], SEG_COUNT, TOKENS, SEG_MOST, 1)), jnp.arange(TOKENS), side="right").astype(jnp.int32),
    }


def attend_block(q_block, k_win, v_win, q_seg, k_seg, q_frame, k_frame):
    scale = 1.0 / (HD ** 0.5)
    scores = jnp.einsum("qhd,khd->hqk", q_block.astype(jnp.float32), k_win.astype(jnp.float32)) * scale
    mask = (q_seg[:, None] == k_seg[None, :]) & (k_frame[None, :] <= q_frame[:, None])
    scores = jnp.where(mask[None], scores, -jnp.inf)
    top = jnp.max(scores, axis=-1)
    expo = jnp.exp(scores - top[..., None])
    total = jnp.sum(expo, axis=-1)
    weights = expo.astype(jnp.bfloat16)
    acc = jnp.einsum("hqk,khd->qhd", weights.astype(jnp.float32), v_win.astype(jnp.float32))
    out = acc / jnp.transpose(total)[:, :, None]
    return out.astype(jnp.bfloat16), top + jnp.log(total)


def reference(queries, keys, values, segment_ids):
    margin = (REACH - 1) * TOK_DEV
    q_all = queries.reshape(TOKENS, H, HD)
    k_pad = jnp.concatenate([jnp.zeros((margin, H, HD), keys.dtype), keys.reshape(TOKENS, H, HD)], axis=0)
    v_pad = jnp.concatenate([jnp.zeros((margin, H, HD), values.dtype), values.reshape(TOKENS, H, HD)], axis=0)
    s_pad = jnp.concatenate([jnp.full((margin,), -1, jnp.int32), segment_ids.astype(jnp.int32)], axis=0)

    def one_block(block):
        start = (block * TOK_DEV).astype(jnp.int32)
        q_block = lax.dynamic_slice_in_dim(q_all, start, TOK_DEV, 0)
        q_seg = lax.dynamic_slice_in_dim(segment_ids, start, TOK_DEV, 0)
        k_win = lax.dynamic_slice_in_dim(k_pad, start, margin + TOK_DEV, 0)
        v_win = lax.dynamic_slice_in_dim(v_pad, start, margin + TOK_DEV, 0)
        k_seg = lax.dynamic_slice_in_dim(s_pad, start, margin + TOK_DEV, 0)
        q_frame = (start + jnp.arange(TOK_DEV, dtype=jnp.int32)) // FRAME
        k_frame = (start - margin + jnp.arange(margin + TOK_DEV, dtype=jnp.int32)) // FRAME
        return attend_block(q_block, k_win, v_win, q_seg, k_seg, q_frame, k_frame)

    outs, sums = lax.map(one_block, jnp.arange(TOKENS // TOK_DEV, dtype=jnp.int32))
    attended = outs.reshape(TOKENS, H * HD)
    log_sum = jnp.transpose(sums, (1, 0, 2)).reshape(H, TOKENS)
    return attended, log_sum
```

```python
import functools
import math

import jax
import jax.numpy as jnp
from jax import lax
from jax.experimental import pallas as pl
from jax.experimental.pallas import tpu as pltpu
from jax.sharding import PartitionSpec as P

T = 128
HALF = T // 2
D = 128
HIDDEN = -1e30
SCALE = 1.0 / math.sqrt(D)
C2 = SCALE / math.log(2.0)
LN2 = math.log(2.0)
MESH = pl.DeviceIdType.MESH
F32 = jnp.float32
BF16 = jnp.bfloat16

QG = 2
OG = 4
LATE = 3


def wide(h):
    return pl.ds(pl.multiple_of(h * D, D), D)


def attend(q, k, v, bias):
    s = lax.dot_general(q, k, (((1,), (1,)), ((), ())), preferred_element_type=F32) + bias
    top = jnp.max(s, axis=1, keepdims=True)
    p = jnp.exp2((s - top) * C2).astype(BF16)
    ext = jnp.concatenate([v, jnp.ones(v.shape, BF16)], axis=1)
    o = lax.dot_general(p, ext, (((1,), (0,)), ((), ())), preferred_element_type=F32)
    total = o[:, D:]
    return o[:, :D] / total, top * C2 + jnp.log2(total)


def kernel(
    n,
    ncp,
    nh,
    q_ref,
    k_ref,
    v_ref,
    id_ref,
    out_ref,
    sum_ref,
    ids,
    q2,
    k2,
    v2,
    qg,
    qf,
    ek,
    ev,
    m_send,
    m_recv,
    l_send,
    l_recv,
    lse_send,
    lse_recv,
    bias_g,
    bias_f,
    bias_o,
    o_loc,
    s_loc,
    stage,
    sums,
    sums_in,
    id_ss,
    id_rs,
    lo_s,
    sib_ss,
    sib_rs,
    e_ss,
    e_rs,
    q_ss,
    qg_rs,
    qf_rs,
    m_ss,
    m_rs,
    l_ss,
    l_rs,
    lse_ss,
    lse_rs,
    out_s,
    oo_ss,
    oo_rs,
    sum_ss,
    sum_rs,
):
    w = nh * D
    ng = nh // QG
    no = nh // OG
    me = lax.axis_index("grp") * ncp + lax.axis_index("cp")
    core = lax.rem(me, 2)
    first = me - core
    other = 1 - core

    def at(i):
        i = lax.rem(i + n, n)
        return (i // ncp, lax.rem(i, ncp))

    sib = at(first + other)
    right = [at(first + 2), at(first + 3)]
    left = [at(first - 2), at(first - 1)]
    ahead = at(me + 2)

    def remote(src, dst, ss, rs, to):
        return pltpu.make_async_remote_copy(
            src_ref=src, dst_ref=dst, send_sem=ss, recv_sem=rs, device_id=to, device_id_type=MESH
        )

    barrier = pltpu.get_barrier_semaphore()
    for to in (sib, *right, *left):
        pl.semaphore_signal(barrier, inc=1, device_id=to, device_id_type=MESH)

    mine = pl.ds(pl.multiple_of(core * w, D), w)
    its = pl.ds(pl.multiple_of(other * w, D), w)
    my_rows = pl.ds(pl.multiple_of(core * T, T), T)
    local = [
        pltpu.make_async_copy(a.at[:, mine], b.at[my_rows, :], lo_s.at[i])
        for i, (a, b) in enumerate(((k_ref, k2), (v_ref, v2), (q_ref, q2)))
    ]
    for cp in local:
        cp.start()
    pl.semaphore_wait(barrier, 5)

    id_sends = []
    for i, (to, slot) in enumerate(
        (
            (sib, 2 + core),
            (right[0], core),
            (right[1], core),
            (left[0], 4 + core),
            (left[1], 4 + core),
        )
    ):
        cp = remote(id_ref, ids.at[slot], id_ss.at[i], id_rs.at[slot], to)
        cp.start()
        id_sends.append(cp)

    def e_copies():
        made = []
        for kk in range(2):
            cols = pl.ds(kk * w, w)
            for i, (a, b) in enumerate(((k_ref, ek), (v_ref, ev))):
                made.append(
                    remote(a.at[pl.ds(HALF, HALF), cols], b, e_ss.at[kk, i], e_rs.at[i], right[kk])
                )
        return made

    def q_copy(g, kk, dst, rs):
        cols = pl.ds(pl.multiple_of((kk * nh + g * QG) * D, D), QG * D)
        here = pl.ds(pl.multiple_of(g * QG * D, D), QG * D)
        return remote(
            q_ref.at[:, cols], dst.at[:, here], q_ss.at[kk, g], rs.at[g], left[kk]
        )

    @pl.when(core == 1)
    def _():
        for g in range(ng):
            for kk in range(2):
                q_copy(g, kk, qg, qg_rs).start()

    sib_sends = [
        remote(a.at[:, its], b.at[my_rows, :], sib_ss.at[i], sib_rs.at[i], sib)
        for i, (a, b) in enumerate(((k_ref, k2), (v_ref, v2), (q_ref, q2)))
    ]
    for cp in sib_sends:
        cp.start()

    @pl.when(core == 1)
    def _():
        for cp in e_copies():
            cp.start()

    ids[2 + core] = id_ref[...]
    for slot in (0, 1, 2 + other, 4, 5):
        remote(id_ref, ids.at[slot], id_ss.at[0], id_rs.at[slot], sib).wait_recv()

    row = [ids[i].astype(F32) for i in range(6)]
    last = [jnp.max(r, axis=1, keepdims=True) for r in row]
    eye = lax.broadcasted_iota(jnp.int32, (T, T), 0) == lax.broadcasted_iota(jnp.int32, (T, T), 1)

    def to_column(r):
        return jnp.sum(jnp.where(eye, jnp.broadcast_to(r, (T, T)), 0.0), axis=1, keepdims=True)

    def to_row(x):
        return jnp.sum(jnp.where(eye, jnp.broadcast_to(x, (T, T)), 0.0), axis=0, keepdims=True)

    def bias_of(q_col, k_row):
        return jnp.where(q_col == k_row, 0.0, HIDDEN)

    behind = jnp.where(last[0] != last[1], row[1], -1.0)
    col = [None, None] + [to_column(row[i]) for i in range(2, 6)]
    for j, keys in enumerate((behind, row[2], row[3])):
        cols = pl.ds(j * T, T)
        bias_f[:, cols] = bias_of(col[4], keys)
        if j:
            bias_g[:, pl.ds((j - 1) * T, T)] = bias_of(col[5], keys)
        bias_o[pl.ds(0, T), cols] = (
            bias_of(col[2], keys) if j < 2 else jnp.full((T, T), HIDDEN, F32)
        )
        bias_o[pl.ds(T, T), cols] = bias_of(col[3], keys)

    kv_row = jnp.broadcast_to(jnp.where(last[2] != last[3], 1.0, 0.0), (1, D))

    for cp in local:
        cp.wait()
    for i, b in enumerate((k2, v2, q2)):
        remote(b.at[my_rows, :], b.at[my_rows, :], sib_ss.at[i], sib_rs.at[i], sib).wait_recv()

    def m_copy(h):
        return remote(m_send.at[h], m_recv.at[h], m_ss.at[h], m_rs.at[h], ahead)

    def l_copy(h):
        return remote(l_send.at[h], l_recv.at[h], l_ss.at[h], l_rs.at[h], ahead)

    def lse_copy(i):
        return remote(lse_send.at[i], lse_recv.at[i], lse_ss.at[i], lse_rs.at[i], ahead)

    def q_wait(g, dst, rs):
        here = pl.ds(pl.multiple_of(g * QG * D, D), QG * D)
        remote(dst.at[:, here], dst.at[:, here], q_ss.at[0, g], rs.at[g], sib).wait_recv()

    def serve_g(g, _):
        q_wait(g, qg, qg_rs)

        @pl.when((core == 0) & (g == LATE))
        def _():
            for gg in range(ng):
                for kk in range(2):
                    q_copy(gg, kk, qf, qf_rs).start()

        kv = kv_row > 0.5
        for u in range(QG):
            h = g * QG + u
            o, lse = attend(qg[:, wide(h)], k2[:, wide(h)], v2[:, wide(h)], bias_g[...])
            lse_send[0, pl.ds(h, 1), :] = jnp.where(kv, HIDDEN, to_row(lse))
            raw = jnp.concatenate(
                [k2[pl.ds(T, HALF), wide(h)], v2[pl.ds(T, HALF), wide(h)]], axis=0
            )
            m_send[h] = jnp.where(kv, raw.astype(F32), o).astype(BF16)
            m_copy(h).start()
        return 0

    lax.fori_loop(0, ng, serve_g, 0)
    lse_copy(0).start()

    remote(ek, ek, e_ss.at[0, 0], e_rs.at[0], sib).wait_recv()
    remote(ev, ev, e_ss.at[0, 1], e_rs.at[1], sib).wait_recv()

    def serve_f(g, _):
        q_wait(g, qf, qf_rs)
        for u in range(QG):
            m_copy(g * QG + u).wait_recv()
        keys, vals = [], []
        for u in range(QG):
            h = g * QG + u
            got = m_recv[h]
            keys.append(jnp.concatenate([got[:HALF], ek[:, wide(h)], k2[:, wide(h)]], axis=0))
            vals.append(jnp.concatenate([got[HALF:], ev[:, wide(h)], v2[:, wide(h)]], axis=0))
        kv = kv_row > 0.5
        for u in range(QG):
            h = g * QG + u
            o, lse = attend(qf[:, wide(h)], keys[u], vals[u], bias_f[...])
            lse_send[1, pl.ds(h, 1), :] = jnp.where(kv, HIDDEN, to_row(lse))
            l_send[h] = o.astype(BF16)
            l_copy(h).start()
        for u in range(QG):
            h = g * QG + u
            o, lse = attend(q2[:, wide(h)], keys[u], vals[u], bias_o[...])
            o_loc[h] = o
            s_loc[h] = lse
        return 0

    lax.fori_loop(0, ng, serve_f, 0)
    lse_copy(1).start()

    def merge(side, h, theirs, got):
        rows = pl.ds(side * T, T)
        here = s_loc[h, rows, :]
        there = to_column(got)
        top = jnp.maximum(here, there)
        a, b = jnp.exp2(here - top), jnp.exp2(there - top)
        both = a + b
        r = 1.0 / both
        out = o_loc[h, rows, :] * (a * r) + theirs.astype(F32) * (b * r)
        stage[side, :, wide(h)] = out.astype(BF16)
        sums[side, pl.ds(h, 1), :] = to_row((top + jnp.log2(both)) * LN2)

    def put(side, g, act):
        cols = pl.ds(g * OG * D, OG * D)
        to = pl.ds(pl.multiple_of(core * w + g * OG * D, D), OG * D)

        @pl.when(core == side)
        def _():
            act(pltpu.make_async_copy(stage.at[side, :, cols], out_ref.at[:, to], out_s.at[g]))

        @pl.when(core != side)
        def _():
            act(
                remote(stage.at[side, :, cols], out_ref.at[:, to], oo_ss.at[g], oo_rs.at[g], sib),
                True,
            )

    def start(cp, far=False):
        cp.start()

    def sent(cp, far=False):
        if far:
            cp.wait_send()
        else:
            cp.wait()

    lse_copy(0).wait_recv()
    for g in range(no):

        def one(i, _):
            h = g * OG + i
            merge(1, h, m_recv[h], lse_recv[0, pl.ds(h, 1), :])
            return 0

        lax.fori_loop(0, OG, one, 0)
        put(1, g, start)

    lse_copy(1).wait_recv()
    for g in range(no):

        def one(i, _):
            h = g * OG + i
            l_copy(h).wait_recv()
            merge(0, h, l_recv[h], lse_recv[1, pl.ds(h, 1), :])
            return 0

        lax.fori_loop(0, OG, one, 0)
        put(0, g, start)

    sum_copy = remote(sums.at[other], sums_in, sum_ss, sum_rs, sib)
    sum_copy.start()

    for cp in id_sends + sib_sends:
        cp.wait_send()

    @pl.when(core == 1)
    def _():
        for cp in e_copies():
            cp.wait_send()
        for g in range(ng):
            for kk in range(2):
                q_copy(g, kk, qg, qg_rs).wait_send()

    @pl.when(core == 0)
    def _():
        for g in range(ng):
            for kk in range(2):
                q_copy(g, kk, qf, qf_rs).wait_send()

    def drain(h, _):
        m_copy(h).wait_send()
        l_copy(h).wait_send()
        return 0

    lax.fori_loop(0, nh, drain, 0)
    lse_copy(0).wait_send()
    lse_copy(1).wait_send()
    sum_copy.wait()

    @pl.when(core == 0)
    def _():
        sum_ref[pl.ds(0, nh), :] = sums[0, pl.ds(0, nh), :]
        sum_ref[pl.ds(nh, nh), :] = sums_in[pl.ds(0, nh), :]

    @pl.when(core == 1)
    def _():
        sum_ref[pl.ds(0, nh), :] = sums_in[pl.ds(0, nh), :]
        sum_ref[pl.ds(nh, nh), :] = sums[1, pl.ds(0, nh), :]

    for g in range(no):
        put(1, g, sent)
        put(0, g, sent)
        to = pl.ds(pl.multiple_of(other * w + g * OG * D, D), OG * D)
        remote(out_ref.at[:, to], out_ref.at[:, to], oo_ss.at[g], oo_rs.at[g], sib).wait_recv()


def shards(mesh, queries, keys, values, segment_ids):
    n, ncp = mesh.size, mesh.shape["cp"]
    width = queries.shape[1]
    heads = width // D
    nh = heads // 2
    ng, no = nh // QG, nh // OG
    w = nh * D
    pad = -(-nh // 8) * 8
    dma = pltpu.SemaphoreType.DMA
    scratch = [
        pltpu.VMEM((6, 1, T), jnp.int32),
        pltpu.VMEM((2 * T, w), BF16),
        pltpu.VMEM((2 * T, w), BF16),
        pltpu.VMEM((2 * T, w), BF16),
        pltpu.VMEM((T, w), BF16),
        pltpu.VMEM((T, w), BF16),
        pltpu.VMEM((HALF, w), BF16),
        pltpu.VMEM((HALF, w), BF16),
        pltpu.VMEM((nh, T, D), BF16),
        pltpu.VMEM((nh, T, D), BF16),
        pltpu.VMEM((nh, T, D), BF16),
        pltpu.VMEM((nh, T, D), BF16),
        pltpu.VMEM((2, pad, T), F32),
        pltpu.VMEM((2, pad, T), F32),
        pltpu.VMEM((T, 2 * T), F32),
        pltpu.VMEM((T, 3 * T), F32),
        pltpu.VMEM((2 * T, 3 * T), F32),
        pltpu.VMEM((nh, 2 * T, D), F32),
        pltpu.VMEM((nh, 2 * T, D), F32),
        pltpu.VMEM((2, T, w), BF16),
        pltpu.VMEM((2, pad, T), F32),
        pltpu.VMEM((pad, T), F32),
        dma((5,)),
        dma((6,)),
        dma((3,)),
        dma((3,)),
        dma((3,)),
        dma((2, 2)),
        dma((2,)),
        dma((2, ng)),
        dma((ng,)),
        dma((ng,)),
        dma((nh,)),
        dma((nh,)),
        dma((nh,)),
        dma((nh,)),
        dma((2,)),
        dma((2,)),
        dma((no,)),
        dma((no,)),
        dma((no,)),
        dma,
        dma,
    ]
    anywhere = pl.BlockSpec(memory_space=pl.ANY)
    vmem = pl.BlockSpec(memory_space=pltpu.VMEM)
    return pl.pallas_call(
        functools.partial(kernel, n, ncp, nh),
        out_shape=(
            jax.ShapeDtypeStruct((T, width), BF16),
            jax.ShapeDtypeStruct((heads, T), F32),
        ),
        in_specs=[anywhere, anywhere, anywhere, vmem],
        out_specs=(anywhere, vmem),
        scratch_shapes=scratch,
        compiler_params=pltpu.CompilerParams(
            collective_id=0, has_side_effects=True, vmem_limit_bytes=48 * 2**20
        ),
        cost_estimate=pl.CostEstimate(
            flops=heads * T * T * D * 20, bytes_accessed=8 * T * width, transcendentals=0
        ),
    )(queries, keys, values, segment_ids.reshape(1, T))


def solution(mesh):
    both = ("grp", "cp")
    return jax.shard_map(
        functools.partial(shards, mesh),
        mesh=mesh,
        in_specs=(P(both, None), P(both, None), P(both, None), P(both)),
        out_specs=(P(both, None), P(None, both)),
        check_vma=False,
    )
```

```python
import functools
import math

import jax
import jax.numpy as jnp
from jax import lax
from jax.experimental import pallas as pl
from jax.experimental.pallas import tpu as pltpu
from jax.sharding import PartitionSpec as P

T = 128
HALF = T // 2
PART = T // 4
D = 128
HIDDEN = -1e30
C2 = 1.0 / math.sqrt(D) / math.log(2.0)
LN2 = math.log(2.0)
MESH = pl.DeviceIdType.MESH
F32 = jnp.float32
BF16 = jnp.bfloat16

QG = 2
OG = 4
LATE = 3


def wide(h):
    return pl.ds(pl.multiple_of(h * D, D), D)


def scores(q, k, bias):
    return lax.dot_general(q, k, (((1,), (1,)), ((), ())), preferred_element_type=F32) + bias


def weigh(p, v):
    ext = jnp.concatenate([v, jnp.ones(v.shape, BF16)], axis=1)
    return lax.dot_general(p, ext, (((1,), (0,)), ((), ())), preferred_element_type=F32)


def attend(q, k, v, bias):
    s = scores(q, k, bias)
    top = jnp.max(s, axis=1, keepdims=True)
    o = weigh(jnp.exp2((s - top) * C2).astype(BF16), v)
    return o[:, :D] / o[:, D:], top * C2 + jnp.log2(o[:, D:])


def kernel(
    n,
    ncp,
    nh,
    q_ref,
    k_ref,
    v_ref,
    id_ref,
    out_ref,
    sum_ref,
    ids,
    q2,
    k2,
    v2,
    qg,
    qf,
    ek,
    ev,
    m_send,
    m_recv,
    l_send,
    l_recv,
    lse_send,
    lse_recv,
    bias_g,
    bias_f,
    bias_o,
    bias_b,
    raw,
    tops,
    o_loc,
    s_loc,
    stage,
    sums,
    go,
    id_ss,
    id_rs,
    lo_s,
    sib_ss,
    sib_rs,
    e_ss,
    e_rs,
    qg_ss,
    qg_rs,
    qf_ss,
    qf_rs,
    m_ss,
    m_rs,
    l_ss,
    l_rs,
    lse_ss,
    lse_rs,
    oo_ss,
    oo_rs,
    sum_ss,
    sum_rs,
):
    w = nh * D
    ng = nh // QG
    no = nh // OG
    me = lax.axis_index("grp") * ncp + lax.axis_index("cp")
    core = lax.rem(me, 2)
    first = me - core
    other = 1 - core
    has_left = first > 0
    has_right = first < n - 2

    def at(i):
        i = lax.rem(i + n, n)
        return (i // ncp, lax.rem(i, ncp))

    sib = at(first + other)
    right = [at(first + 2), at(first + 3)]
    left = [at(first - 2), at(first - 1)]
    ahead = at(me + 2)

    def remote(src, dst, ss, rs, to):
        return pltpu.make_async_remote_copy(
            src_ref=src, dst_ref=dst, send_sem=ss, recv_sem=rs, device_id=to, device_id_type=MESH
        )

    def greet(sem, to):
        pl.semaphore_signal(sem, inc=1, device_id=to, device_id_type=MESH)

    def arrived(dst, rs):
        remote(dst, dst, sum_ss.at[0], rs, sib).wait_recv()

    barrier = pltpu.get_barrier_semaphore()
    greet(barrier, sib)

    @pl.when(has_left)
    def _():
        greet(barrier, left[0])
        greet(barrier, left[1])

    mine = pl.ds(pl.multiple_of(core * w, D), w)
    its = pl.ds(pl.multiple_of(other * w, D), w)
    my_rows = pl.ds(pl.multiple_of(core * T, T), T)
    its_rows = pl.ds(pl.multiple_of(other * T, T), T)
    trio = ((k_ref, k2), (v_ref, v2), (q_ref, q2))
    local = [
        pltpu.make_async_copy(a.at[:, mine], b.at[my_rows, :], lo_s.at[i])
        for i, (a, b) in enumerate(trio)
    ]
    local.append(pltpu.make_async_copy(id_ref, ids.at[2 + core], lo_s.at[3]))
    for cp in local:
        cp.start()
    pl.semaphore_wait(barrier, 1 + 2 * has_right.astype(jnp.int32))

    @pl.when(has_right)
    def _():
        greet(go, right[0])
        greet(go, right[1])

    id_sib = remote(id_ref, ids.at[2 + core], id_ss.at[0], id_rs.at[2 + core], sib)
    id_right = [
        remote(id_ref, ids.at[core], id_ss.at[1 + i], id_rs.at[core], right[i]) for i in range(2)
    ]
    id_left = [
        remote(id_ref, ids.at[4 + core], id_ss.at[3 + i], id_rs.at[4 + core], left[i])
        for i in range(2)
    ]
    sib_sends = [
        remote(a.at[:, its], b.at[my_rows, :], sib_ss.at[i], sib_rs.at[i], sib)
        for i, (a, b) in enumerate(trio)
    ]

    def e_copies():
        return [
            remote(
                a.at[pl.ds(T - PART, PART), pl.ds(kk * w, w)], b, e_ss.at[kk, i], e_rs.at[i], right[kk]
            )
            for kk in range(2)
            for i, (a, b) in enumerate(((k_ref, ek), (v_ref, ev)))
        ]

    def q_cols(g):
        return pl.ds(pl.multiple_of(g * QG * D, D), QG * D)

    def qg_copy(g, kk):
        cols = pl.ds(pl.multiple_of((kk * nh + g * QG) * D, D), QG * D)
        return remote(
            q_ref.at[:, cols], qg.at[:, q_cols(g)], qg_ss.at[kk, g], qg_rs.at[g], left[kk]
        )

    def qf_copy(part, g, kk):
        cols = pl.ds(pl.multiple_of((kk * nh + g * QG) * D, D), QG * D)
        rows = pl.ds(part * HALF, HALF)
        return remote(
            q_ref.at[rows, cols],
            qf.at[rows, q_cols(g)],
            qf_ss.at[part, kk, g],
            qf_rs.at[part, g],
            left[kk],
        )

    sib_sends[0].start()

    @pl.when(has_right)
    def _():
        id_right[0].start()
        id_right[1].start()

        @pl.when(core == 1)
        def _():
            for cp in e_copies():
                cp.start()

    id_sib.start()
    sib_sends[1].start()

    @pl.when(has_left)
    def _():
        pl.semaphore_wait(go, 2)
        id_left[0].start()
        id_left[1].start()

        @pl.when(core == 1)
        def _():
            for g in range(ng):
                for kk in range(2):
                    qg_copy(g, kk).start()

    sib_sends[2].start()

    @pl.when(jnp.logical_not(has_left))
    def _():
        ids[0] = jnp.full((1, T), -1, jnp.int32)
        ids[1] = jnp.full((1, T), -1, jnp.int32)
        ek[...] = jnp.zeros(ek.shape, BF16)
        ev[...] = jnp.zeros(ev.shape, BF16)
        m_recv[...] = jnp.zeros(m_recv.shape, BF16)
        l_recv[...] = jnp.zeros(l_recv.shape, BF16)
        lse_recv[...] = jnp.full(lse_recv.shape, HIDDEN, F32)

    @pl.when(jnp.logical_not(has_right))
    def _():
        ids[4] = jnp.full((1, T), -2, jnp.int32)
        ids[5] = jnp.full((1, T), -2, jnp.int32)

    def iota(shape, axis):
        return lax.broadcasted_iota(jnp.int32, shape, axis)

    eye = iota((T, T), 0) == iota((T, T), 1)
    eyes = [iota((HALF, T), 0) + HALF * i == iota((HALF, T), 1) for i in range(2)]

    def to_column(r, like):
        return jnp.sum(
            jnp.where(like, jnp.broadcast_to(r, like.shape), 0.0), axis=1, keepdims=True
        )

    def to_row(x, like):
        return jnp.sum(jnp.where(like, x, 0.0), axis=0, keepdims=True)

    def bias_of(q_col, k_row):
        return jnp.where(q_col == k_row, 0.0, HIDDEN)

    arrived(ids.at[2 + other], id_rs.at[2 + other])
    local[3].wait()
    own = [ids[2].astype(F32), ids[3].astype(F32)]
    own_col = [to_column(r, eye) for r in own]
    for i in range(2):
        for j in range(2):
            bias_o[pl.ds(i * T, T), pl.ds(j * T, T)] = (
                bias_of(own_col[i], own[j]) if j <= i else jnp.full((T, T), HIDDEN, F32)
            )

    last = [jnp.max(r, axis=1, keepdims=True) for r in own]
    kv_row = jnp.broadcast_to(jnp.where(last[0] != last[1], 1.0, 0.0), (1, D))

    @pl.when(has_right)
    def _():
        arrived(ids.at[4], id_rs.at[4])
        arrived(ids.at[5], id_rs.at[5])

    its_col = [to_column(ids[4 + i].astype(F32), eye) for i in range(2)]
    for j in range(2):
        bias_g[:, pl.ds(j * T, T)] = bias_of(its_col[1], own[j])
        bias_f[:, pl.ds((j + 1) * T, T)] = bias_of(its_col[0], own[j])

    for cp in local[:3]:
        cp.wait()
    for i, b in enumerate((k2, v2, q2)):
        arrived(b.at[its_rows, :], sib_rs.at[i])

    def m_copy(h):
        return remote(m_send.at[h], m_recv.at[h], m_ss.at[h], m_rs.at[h], ahead)

    def l_copy(part, h):
        return remote(
            l_send.at[part, h], l_recv.at[part, h], l_ss.at[part, h], l_rs.at[part, h], ahead
        )

    def lse_copy(i):
        return remote(lse_send.at[i], lse_recv.at[i], lse_ss.at[i], lse_rs.at[i], ahead)

    def step_g(g, _):
        @pl.when(has_right)
        def _():
            arrived(qg.at[:, q_cols(g)], qg_rs.at[g])

        @pl.when(has_left & (core == 0) & (g == LATE))
        def _():
            for part in (1, 0):
                for gg in range(ng):
                    for kk in range(2):
                        qf_copy(part, gg, kk).start()

        kv = kv_row > 0.5
        for u in range(QG):
            h = g * QG + u
            o, lse = attend(qg[:, wide(h)], k2[:, wide(h)], v2[:, wide(h)], bias_g[...])
            lse_send[0, pl.ds(h, 1), :] = jnp.where(kv, HIDDEN, to_row(lse, eye))
            rows = pl.ds(T + PART, HALF)
            there = jnp.concatenate([k2[rows, wide(h)], v2[rows, wide(h)]], axis=0)
            m_send[h] = jnp.where(kv, there.astype(F32), o).astype(BF16)

            @pl.when(has_right)
            def _():
                m_copy(h).start()

        for u in range(QG):
            h = g * QG + u
            s = scores(q2[:, wide(h)], k2[:, wide(h)], bias_o[...])
            top = jnp.max(s, axis=1, keepdims=True)
            raw[h] = weigh(jnp.exp2((s - top) * C2).astype(BF16), v2[:, wide(h)])
            tops[h] = jnp.broadcast_to(top, (2 * T, D))
        return 0

    lax.fori_loop(0, ng, step_g, 0)

    @pl.when(has_right)
    def _():
        lse_copy(0).start()

    @pl.when(has_left)
    def _():
        arrived(ids.at[0], id_rs.at[0])
        arrived(ids.at[1], id_rs.at[1])
        arrived(ek, e_rs.at[0])
        arrived(ev, e_rs.at[1])

    before = [ids[i].astype(F32) for i in range(2)]
    behind_last = [jnp.max(r, axis=1, keepdims=True) for r in before]
    behind = jnp.where(behind_last[0] != behind_last[1], before[1], -1.0)
    for i in range(2):
        bias_b[pl.ds(i * T, T), :] = bias_of(own_col[i], behind)
    late = (iota((T, T), 0) >= HALF) & (iota((T, T), 1) < PART)
    bias_f[:, pl.ds(0, T)] = jnp.where(late, HIDDEN, bias_of(its_col[0], behind))

    def step_f1(g, _):
        @pl.when(has_right)
        def _():
            arrived(qf.at[pl.ds(HALF, HALF), q_cols(g)], qf_rs.at[1, g])

        @pl.when(has_left)
        def _():
            for u in range(QG):
                arrived(m_recv.at[g * QG + u], m_rs.at[g * QG + u])

        kv = kv_row > 0.5
        none = jnp.zeros((PART, D), BF16)
        for u in range(QG):
            h = g * QG + u
            got = m_recv[h]
            keys = jnp.concatenate([none, got[:HALF], ek[:, wide(h)], k2[:, wide(h)]], axis=0)
            vals = jnp.concatenate([none, got[HALF:], ev[:, wide(h)], v2[:, wide(h)]], axis=0)
            o, lse = attend(
                qf[pl.ds(HALF, HALF), wide(h)], keys, vals, bias_f[pl.ds(HALF, HALF), :]
            )
            lse_send[1, pl.ds(h, 1), :] = jnp.where(kv, HIDDEN, to_row(lse, eyes[1]))
            rows = pl.ds(T, PART)
            there = jnp.concatenate([k2[rows, wide(h)], v2[rows, wide(h)]], axis=0)
            l_send[1, h] = jnp.where(kv, there.astype(F32), o).astype(BF16)

            @pl.when(has_right)
            def _():
                l_copy(1, h).start()

        return 0

    lax.fori_loop(0, ng, step_f1, 0)

    @pl.when(has_right)
    def _():
        lse_copy(1).start()

    def step_f0(g, _):
        @pl.when(has_right)
        def _():
            arrived(qf.at[pl.ds(0, HALF), q_cols(g)], qf_rs.at[0, g])

        @pl.when(has_left)
        def _():
            for u in range(QG):
                arrived(l_recv.at[1, g * QG + u], l_rs.at[1, g * QG + u])

        kv = kv_row > 0.5
        keys, vals = [], []
        for u in range(QG):
            h = g * QG + u
            low, got = l_recv[1, h], m_recv[h]
            keys.append(jnp.concatenate([low[:PART], got[:HALF], ek[:, wide(h)]], axis=0))
            vals.append(jnp.concatenate([low[PART:], got[HALF:], ev[:, wide(h)]], axis=0))
        for u in range(QG):
            h = g * QG + u
            o, lse = attend(
                qf[pl.ds(0, HALF), wide(h)],
                jnp.concatenate([keys[u], k2[:, wide(h)]], axis=0),
                jnp.concatenate([vals[u], v2[:, wide(h)]], axis=0),
                bias_f[pl.ds(0, HALF), :],
            )
            lse_send[2, pl.ds(h, 1), :] = jnp.where(kv, HIDDEN, to_row(lse, eyes[0]))
            l_send[0, h] = o.astype(BF16)

            @pl.when(has_right)
            def _():
                l_copy(0, h).start()

        for u in range(QG):
            h = g * QG + u
            s = scores(q2[:, wide(h)], keys[u], bias_b[...])
            old = tops[h]
            top = jnp.maximum(old, jnp.max(s, axis=1, keepdims=True))
            fade = jnp.exp2((old - top) * C2)
            new = weigh(jnp.exp2((s - top) * C2).astype(BF16), vals[u])
            total = raw[h, :, pl.ds(D, D)] * fade + new[:, D:]
            o_loc[h] = (raw[h, :, pl.ds(0, D)] * fade + new[:, :D]) / total
            s_loc[h] = top * C2 + jnp.log2(total)
        return 0

    lax.fori_loop(0, ng, step_f0, 0)

    @pl.when(has_right)
    def _():
        lse_copy(2).start()

    def merge(side, start, size, h, theirs, got, like):
        rows = pl.ds(side * T + start, size)
        here = s_loc[h, rows, :]
        there = to_column(got, like)
        top = jnp.maximum(here, there)
        a, b = jnp.exp2(here - top), jnp.exp2(there - top)
        both = a + b
        r = 1.0 / both
        out = o_loc[h, rows, :] * (a * r) + theirs.astype(F32) * (b * r)
        stage[side, pl.ds(start, size), wide(h)] = out.astype(BF16)
        return to_row((top + jnp.log2(both)) * LN2, like)

    def put(slot, side, start, size, g, heads, act):
        rows = pl.ds(start, size)
        cols = pl.ds(g * heads * D, heads * D)
        to = pl.ds(pl.multiple_of(core * w + g * heads * D, D), heads * D)
        src, dst = stage.at[side, rows, cols], out_ref.at[rows, to]

        @pl.when(core == side)
        def _():
            act(pltpu.make_async_copy(src, dst, oo_ss.at[slot]), False)

        @pl.when(core != side)
        def _():
            act(remote(src, dst, oo_ss.at[slot], oo_rs.at[slot], sib), True)

    def begin(cp, far):
        cp.start()

    def sent(cp, far):
        if far:
            cp.wait_send()
        else:
            cp.wait()

    puts = [(0, 1, 0, T, 0, nh), (1, 0, HALF, HALF, 0, nh)] + [
        (2 + g, 0, 0, HALF, g, OG) for g in range(no)
    ]

    @pl.when(has_left)
    def _():
        arrived(lse_recv.at[0], lse_rs.at[0])
        arrived(lse_recv.at[1], lse_rs.at[1])

    def step_e(h, _):
        sums[1, pl.ds(h, 1), :] = merge(
            1, 0, T, h, m_recv[h], lse_recv[0, pl.ds(h, 1), :], eye
        )
        sums[0, pl.ds(h, 1), :] = merge(
            0, HALF, HALF, h, l_recv[1, h], lse_recv[1, pl.ds(h, 1), :], eyes[1]
        )
        return 0

    lax.fori_loop(0, nh, step_e, 0)
    put(*puts[0], begin)
    put(*puts[1], begin)

    @pl.when(has_left)
    def _():
        arrived(lse_recv.at[2], lse_rs.at[2])

    for g in range(no):

        def step_d(i, _):
            h = g * OG + i

            @pl.when(has_left)
            def _():
                arrived(l_recv.at[0, h], l_rs.at[0, h])

            sums[0, pl.ds(h, 1), :] += merge(
                0, 0, HALF, h, l_recv[0, h], lse_recv[2, pl.ds(h, 1), :], eyes[0]
            )
            return 0

        lax.fori_loop(0, OG, step_d, 0)
        put(*puts[2 + g], begin)

    own_sum = pltpu.make_async_copy(sums.at[core], sum_ref.at[core], sum_ss.at[0])
    far_sum = remote(sums.at[other], sum_ref.at[core], sum_ss.at[1], sum_rs, sib)
    own_sum.start()
    far_sum.start()

    id_sib.wait_send()
    for cp in sib_sends:
        cp.wait_send()

    @pl.when(has_right)
    def _():
        for cp in id_right:
            cp.wait_send()

        @pl.when(core == 1)
        def _():
            for cp in e_copies():
                cp.wait_send()

        def drain(h, _):
            m_copy(h).wait_send()
            l_copy(1, h).wait_send()
            l_copy(0, h).wait_send()
            return 0

        lax.fori_loop(0, nh, drain, 0)
        for i in range(3):
            lse_copy(i).wait_send()

    @pl.when(has_left)
    def _():
        for cp in id_left:
            cp.wait_send()

        @pl.when(core == 1)
        def _():
            for g in range(ng):
                for kk in range(2):
                    qg_copy(g, kk).wait_send()

        @pl.when(core == 0)
        def _():
            for g in range(ng):
                for kk in range(2):
                    qf_copy(0, g, kk).wait_send()
                    qf_copy(1, g, kk).wait_send()

    for p in puts:
        put(*p, sent)
    own_sum.wait()
    far_sum.wait_send()
    arrived(sum_ref.at[other], sum_rs)
    for slot, side, start, size, g, heads in puts:

        @pl.when(core == side)
        def _():
            to = pl.ds(pl.multiple_of(other * w + g * heads * D, D), heads * D)
            arrived(out_ref.at[pl.ds(start, size), to], oo_rs.at[slot])


CHUNKS = 8


def finish(nh, out_in, sum_in, out_ref, sum_ref, sem):
    size = out_in.shape[0] // CHUNKS
    cps = [
        pltpu.make_async_copy(
            out_in.at[pl.ds(i * size, size), :], out_ref.at[pl.ds(i * size, size), :], sem.at[i]
        )
        for i in range(CHUNKS)
    ]
    for cp in cps:
        cp.start()
    for i in range(2):
        sum_ref[pl.ds(i * nh, nh), :] = sum_in[i, pl.ds(0, nh), :]
    for cp in cps:
        cp.wait()


def shards(mesh, queries, keys, values, segment_ids):
    n, ncp = mesh.size, mesh.shape["cp"]
    width = queries.shape[1]
    heads = width // D
    nh = heads // 2
    ng, no = nh // QG, nh // OG
    w = nh * D
    pad = -(-nh // 8) * 8
    dma = pltpu.SemaphoreType.DMA
    scratch = [
        pltpu.VMEM((6, 1, T), jnp.int32),
        pltpu.VMEM((2 * T, w), BF16),
        pltpu.VMEM((2 * T, w), BF16),
        pltpu.VMEM((2 * T, w), BF16),
        pltpu.VMEM((T, w), BF16),
        pltpu.VMEM((T, w), BF16),
        pltpu.VMEM((PART, w), BF16),
        pltpu.VMEM((PART, w), BF16),
        pltpu.VMEM((nh, T, D), BF16),
        pltpu.VMEM((nh, T, D), BF16),
        pltpu.VMEM((2, nh, HALF, D), BF16),
        pltpu.VMEM((2, nh, HALF, D), BF16),
        pltpu.VMEM((3, pad, T), F32),
        pltpu.VMEM((3, pad, T), F32),
        pltpu.VMEM((T, 2 * T), F32),
        pltpu.VMEM((T, 3 * T), F32),
        pltpu.VMEM((2 * T, 2 * T), F32),
        pltpu.VMEM((2 * T, T), F32),
        pltpu.VMEM((nh, 2 * T, 2 * D), F32),
        pltpu.VMEM((nh, 2 * T, D), F32),
        pltpu.VMEM((nh, 2 * T, D), F32),
        pltpu.VMEM((nh, 2 * T, D), F32),
        pltpu.VMEM((2, T, w), BF16),
        pltpu.VMEM((2, pad, T), F32),
        pltpu.SemaphoreType.REGULAR,
        dma((5,)),
        dma((6,)),
        dma((4,)),
        dma((3,)),
        dma((3,)),
        dma((2, 2)),
        dma((2,)),
        dma((2, ng)),
        dma((ng,)),
        dma((2, 2, ng)),
        dma((2, ng)),
        dma((nh,)),
        dma((nh,)),
        dma((2, nh)),
        dma((2, nh)),
        dma((3,)),
        dma((3,)),
        dma((2 + no,)),
        dma((2 + no,)),
        dma((2,)),
        dma,
    ]
    anywhere = pl.BlockSpec(memory_space=pl.ANY)
    vmem = pl.BlockSpec(memory_space=pltpu.VMEM)
    out, sums = pl.pallas_call(
        functools.partial(kernel, n, ncp, nh),
        out_shape=(
            jax.ShapeDtypeStruct((T, width), BF16),
            jax.ShapeDtypeStruct((2, pad, T), F32),
        ),
        in_specs=[anywhere, anywhere, anywhere, anywhere],
        out_specs=(anywhere, anywhere),
        scratch_shapes=scratch,
        compiler_params=pltpu.CompilerParams(
            collective_id=0, has_side_effects=True, vmem_limit_bytes=53 * 2**20
        ),
        cost_estimate=pl.CostEstimate(
            flops=heads * T * T * D * 20, bytes_accessed=8 * T * width, transcendentals=0
        ),
    )(queries, keys, values, segment_ids.reshape(1, T))
    return pl.pallas_call(
        functools.partial(finish, nh),
        out_shape=(
            jax.ShapeDtypeStruct((T, width), BF16),
            jax.ShapeDtypeStruct((heads, T), F32),
        ),
        in_specs=[anywhere, vmem],
        out_specs=(anywhere, vmem),
        scratch_shapes=[dma((CHUNKS,))],
        compiler_params=pltpu.CompilerParams(vmem_limit_bytes=48 * 2**20),
    )(out, sums)


def solution(mesh):
    both = ("grp", "cp")
    return jax.shard_map(
        functools.partial(shards, mesh),
        mesh=mesh,
        in_specs=(P(both, None), P(both, None), P(both, None), P(both)),
        out_specs=(P(both, None), P(None, both)),
        check_vma=False,
    )
```

```python
import functools
import math

import jax
import jax.numpy as jnp
from jax import lax
from jax.experimental import pallas as pl
from jax.experimental.pallas import tpu as pltpu
from jax.sharding import PartitionSpec as P

T = 128
HALF = T // 2
PART = T // 4
G = 96
MID = G // 2
END = T - PART - MID
D = 128
HIDDEN = -1e30
C2 = 1.0 / math.sqrt(D) / math.log(2.0)
LN2 = math.log(2.0)
MESH = pl.DeviceIdType.MESH
F32 = jnp.float32
BF16 = jnp.bfloat16

QG = 2
OG = 4
LINE = 16
AHEAD = 6
TWO = 2
PUMP = 12
MORE = 2
LINE = 16


def wide(h):
    return pl.ds(pl.multiple_of(h * D, D), D)


def scores(q, k, bias):
    return lax.dot_general(q, k, (((1,), (1,)), ((), ())), preferred_element_type=F32) + bias


def weigh(p, v):
    return lax.dot_general(
        p.astype(BF16), v, (((1,), (0,)), ((), ())), preferred_element_type=F32
    )


def attend(q, k, v, bias):
    s = scores(q, k, bias)
    top = jnp.max(s, axis=1, keepdims=True)
    p = jnp.exp2((s - top) * C2)
    total = jnp.sum(p, axis=1, keepdims=True)
    return weigh(p, v) * (1.0 / total), top * C2 + jnp.log2(total)


def kernel(
    n,
    ncp,
    nh,
    q_ref,
    k_ref,
    v_ref,
    id_ref,
    out_ref,
    sum_ref,
    ids,
    q2,
    k2,
    v2,
    qg,
    qf,
    ek,
    ev,
    m_send,
    m_recv,
    l_send,
    l_recv,
    lse_send,
    lse_recv,
    bias_g,
    bias_f,
    bias_o,
    bias_a,
    o_loc,
    s_loc,
    stage,
    sums,
    go,
    id_ss,
    id_rs,
    lo_s,
    sib_ss,
    sib_rs,
    e_ss,
    e_rs,
    q_ss,
    q_rs,
    m_ss,
    m_rs,
    l_ss,
    l_rs,
    lse_ss,
    lse_rs,
    oo_ss,
    oo_rs,
    sum_ss,
    sum_rs,
):
    w = nh * D
    ng = nh // QG
    no = nh // OG
    me = lax.axis_index("grp") * ncp + lax.axis_index("cp")
    core = lax.rem(me, 2)
    first = me - core
    other = 1 - core
    has_left = first > 0
    has_right = first < n - 2
    waits = lax.rem(first, LINE) == 0
    prompt = jnp.logical_not(waits)
    ends = lax.rem(first, LINE) == LINE - 2

    def at(i):
        i = lax.rem(i + n, n)
        return (i // ncp, lax.rem(i, ncp))

    sib = at(first + other)
    right = [at(first + 2), at(first + 3)]
    left = [at(first - 2), at(first - 1)]
    ahead = at(me + 2)
    behind_me = at(me - 2)

    def remote(src, dst, ss, rs, to):
        return pltpu.make_async_remote_copy(
            src_ref=src, dst_ref=dst, send_sem=ss, recv_sem=rs, device_id=to, device_id_type=MESH
        )

    def greet(sem, to):
        pl.semaphore_signal(sem, inc=1, device_id=to, device_id_type=MESH)

    def arrived(dst, rs):
        remote(dst, dst, sum_ss.at[0], rs, sib).wait_recv()

    barrier = pltpu.get_barrier_semaphore()
    greet(barrier, sib)

    @pl.when(has_left)
    def _():
        greet(barrier, left[0])
        greet(barrier, left[1])

    mine = pl.ds(pl.multiple_of(core * w, D), w)
    its = pl.ds(pl.multiple_of(other * w, D), w)
    my_rows = pl.ds(pl.multiple_of(core * T, T), T)
    its_rows = pl.ds(pl.multiple_of(other * T, T), T)
    trio = ((k_ref, k2), (v_ref, v2), (q_ref, q2))
    local = [
        pltpu.make_async_copy(a.at[:, mine], b.at[my_rows, :], lo_s.at[i])
        for i, (a, b) in enumerate(trio)
    ]
    local.append(pltpu.make_async_copy(id_ref, ids.at[2 + core], lo_s.at[3]))
    for cp in local:
        cp.start()
    pl.semaphore_wait(barrier, 1 + 2 * has_right.astype(jnp.int32))

    @pl.when(has_right)
    def _():
        greet(go, right[0])
        greet(go, right[1])

    id_sib = remote(id_ref, ids.at[2 + core], id_ss.at[0], id_rs.at[2 + core], sib)
    id_right = [
        remote(id_ref, ids.at[core], id_ss.at[1 + i], id_rs.at[core], right[i]) for i in range(2)
    ]
    id_left = [
        remote(id_ref, ids.at[4 + core], id_ss.at[3 + i], id_rs.at[4 + core], left[i])
        for i in range(2)
    ]
    sib_sends = [
        remote(a.at[:, its], b.at[my_rows, :], sib_ss.at[i], sib_rs.at[i], sib)
        for i, (a, b) in enumerate(trio)
    ]

    def e_copy(i):
        a, b = ((k2, ek), (v2, ev))[i]
        return remote(a.at[pl.ds(2 * T - END, END), :], b, e_ss.at[i], e_rs.at[i], ahead)

    def q_cols(g):
        return pl.ds(pl.multiple_of(g * QG * D, D), QG * D)

    pieces = ((T, qg, 0, G), (HALF, qf, HALF, HALF), (0, qf, 0, HALF))

    def q_copy(piece, g):
        start, to, row, size = pieces[piece]
        return remote(
            q2.at[pl.ds(start, size), q_cols(g)],
            to.at[pl.ds(row, size), q_cols(g)],
            q_ss.at[piece, g],
            q_rs.at[piece, g],
            behind_me,
        )

    def q_arrived(piece, g):
        _, to, row, size = pieces[piece]
        arrived(to.at[pl.ds(row, size), q_cols(g)], q_rs.at[piece, g])

    def q_next(i):
        for piece in range(3):

            @pl.when(has_left & (i >= piece * ng) & (i < (piece + 1) * ng))
            def _():
                q_copy(piece, i - piece * ng).start()

    sib_sends[2].start()
    id_sib.start()
    sib_sends[0].start()
    sib_sends[1].start()

    @pl.when(has_right)
    def _():
        id_right[0].start()
        id_right[1].start()

    @pl.when(jnp.logical_not(has_left))
    def _():
        ids[0] = jnp.full((1, T), -1, jnp.int32)
        ids[1] = jnp.full((1, T), -1, jnp.int32)
        ek[...] = jnp.zeros(ek.shape, BF16)
        ev[...] = jnp.zeros(ev.shape, BF16)
        m_recv[...] = jnp.zeros(m_recv.shape, BF16)
        l_recv[...] = jnp.zeros(l_recv.shape, BF16)
        lse_recv[...] = jnp.full(lse_recv.shape, HIDDEN, F32)

    @pl.when(jnp.logical_not(has_right))
    def _():
        ids[4] = jnp.full((1, T), -2, jnp.int32)
        ids[5] = jnp.full((1, T), -2, jnp.int32)

    def iota(shape, axis):
        return lax.broadcasted_iota(jnp.int32, shape, axis)

    eye = iota((T, T), 0) == iota((T, T), 1)
    eyes = [iota((HALF, T), 0) + HALF * i == iota((HALF, T), 1) for i in range(2)]
    eye_g = iota((G, T), 0) == iota((G, T), 1)

    def to_column(r, like):
        return jnp.sum(
            jnp.where(like, jnp.broadcast_to(r, like.shape), 0.0), axis=1, keepdims=True
        )

    def to_row(x, like):
        return jnp.sum(jnp.where(like, x, 0.0), axis=0, keepdims=True)

    def bias_of(q_col, k_row):
        return jnp.where(q_col == k_row, 0.0, HIDDEN)

    def have(i):
        local[i].wait()
        arrived(trio[i][1].at[its_rows, :], sib_rs.at[i])

    have(0)
    have(1)

    @pl.when(has_right)
    def _():
        e_copy(0).start()
        e_copy(1).start()

    have(2)
    arrived(ids.at[2 + other], id_rs.at[2 + other])
    local[3].wait()
    own = [ids[2].astype(F32), ids[3].astype(F32)]
    own_col = [to_column(r, eye) for r in own]
    for i in range(2):
        for j in range(2):
            bias_o[pl.ds(i * T, T), pl.ds((j + 1) * T, T)] = (
                bias_of(own_col[i], own[j]) if j <= i else jnp.full((T, T), HIDDEN, F32)
            )

    lane = iota((1, T), 1)

    def short(a, b):
        edge = jnp.sum(jnp.where(lane == T - PART - 1, a, 0.0), axis=1, keepdims=True)
        return edge != jnp.max(b, axis=1, keepdims=True)

    kv_row = jnp.broadcast_to(jnp.where(short(*own), 1.0, 0.0), (1, D))

    @pl.when(has_left)
    def _():
        pl.semaphore_wait(go, 2)
        id_left[0].start()
        id_left[1].start()
        for i in range(AHEAD):

            @pl.when(prompt | (i < TWO))
            def _():
                q_copy(i // ng, i % ng).start()

    @pl.when(has_right)
    def _():
        arrived(ids.at[4], id_rs.at[4])
        arrived(ids.at[5], id_rs.at[5])

    its_col = [to_column(ids[4 + i].astype(F32), eye) for i in range(2)]
    for j in range(2):
        bias_g[:, pl.ds(j * T, T)] = bias_of(its_col[1][:G], own[j])
        bias_f[:, pl.ds((j + 1) * T, T)] = bias_of(its_col[0], own[j])

    def m_copy(h):
        return remote(m_send.at[h], m_recv.at[h], m_ss.at[h], m_rs.at[h], ahead)

    def l_copy(part, h):
        return remote(
            l_send.at[part, h], l_recv.at[part, h], l_ss.at[part, h], l_rs.at[part, h], ahead
        )

    def lse_copy(i, g):
        return remote(
            lse_send.at[i, g], lse_recv.at[i, g], lse_ss.at[i, g], lse_rs.at[i, g], ahead
        )

    def step_g(g, _):
        @pl.when(prompt)
        def _():
            q_next(AHEAD + g)

        @pl.when(waits & has_left)
        def _():
            q_copy(0, g).wait_send()
            q_next(TWO + g)

        @pl.when(has_right)
        def _():
            q_arrived(0, g)

        kv = kv_row > 0.5
        for u in range(QG):
            h = g * QG + u
            o, lse = attend(qg[:, wide(h)], k2[:, wide(h)], v2[:, wide(h)], bias_g[...])
            lse_send[0, g, pl.ds(u, 1), :] = jnp.where(kv | (lane >= G), HIDDEN, to_row(lse, eye_g))
            rows = pl.ds(T + PART, MID)
            there = jnp.concatenate([k2[rows, wide(h)], v2[rows, wide(h)]], axis=0)
            m_send[h] = jnp.where(kv, there.astype(F32), o).astype(BF16)

            @pl.when(has_right)
            def _():
                m_copy(h).start()

        @pl.when(has_right)
        def _():
            lse_copy(0, g).start()

        return 0

    lax.fori_loop(0, ng, step_g, 0)

    @pl.when(waits & has_left)
    def _():
        for i in range(TWO + ng, PUMP):
            q_copy((i - TWO) // ng, (i - TWO) % ng).wait_send()
            q_copy(i // ng, i % ng).start()

    @pl.when(has_left)
    def _():
        arrived(ids.at[0], id_rs.at[0])
        arrived(ids.at[1], id_rs.at[1])
        arrived(ek, e_rs.at[0])
        arrived(ev, e_rs.at[1])

    before = [ids[i].astype(F32) for i in range(2)]
    seen = [jnp.where(short(*before), r, -1.0) for r in before]
    behind = seen[1]
    low_keys = jnp.concatenate([seen[0][:, T - PART :], behind[:, :PART]], axis=1)
    for i in range(2):
        rows = pl.ds(i * T, T)
        bias_o[rows, pl.ds(0, T)] = jnp.where(
            iota((T, T), 1) < PART, HIDDEN, bias_of(own_col[i], behind)
        )
        bias_a[rows, :] = bias_of(own_col[i], low_keys)
    late = (iota((T, T), 0) >= HALF) & (iota((T, T), 1) < PART)
    bias_f[:, pl.ds(0, T)] = jnp.where(late, HIDDEN, bias_of(its_col[0], behind))

    def near(h):
        none = jnp.zeros((PART, D), BF16)
        got = m_recv[h]
        keys = jnp.concatenate([none, got[:MID], ek[:, wide(h)], k2[:, wide(h)]], axis=0)
        vals = jnp.concatenate([none, got[MID:], ev[:, wide(h)], v2[:, wide(h)]], axis=0)
        return keys, vals

    def own(h, keys, vals):
        o_loc[h], lse = attend(q2[:, wide(h)], keys, vals, bias_o[...])
        s_loc[h] = jnp.broadcast_to(lse, (2 * T, D))

    def step_f1(g, _):
        @pl.when(waits)
        def _():
            for i in range(MORE):
                q_next(PUMP + g * MORE + i)

        @pl.when(prompt)
        def _():
            q_next(AHEAD + ng + g)

        @pl.when(has_right)
        def _():
            q_arrived(1, g)

        @pl.when(has_left)
        def _():
            for u in range(QG):
                arrived(m_recv.at[g * QG + u], m_rs.at[g * QG + u])

        def reply(u, o, lse):
            h = g * QG + u
            kv = kv_row > 0.5
            lse_send[1, g, pl.ds(u, 1), :] = jnp.where(
                kv | (lane < HALF), HIDDEN, to_row(lse, eyes[1])
            )
            rows = pl.ds(T, PART)
            there = jnp.concatenate([k2[rows, wide(h)], v2[rows, wide(h)]], axis=0)
            l_send[1, h] = jnp.where(kv, there.astype(F32), o).astype(BF16)

            @pl.when(has_right)
            def _():
                l_copy(1, h).start()

        @pl.when(jnp.logical_not(ends))
        def _():
            for u in range(QG):
                h = g * QG + u
                q = jnp.concatenate([qf[pl.ds(HALF, HALF), wide(h)], q2[:, wide(h)]], axis=0)
                bias = jnp.concatenate([bias_f[pl.ds(HALF, HALF), :], bias_o[...]], axis=0)
                o, lse = attend(q, *near(h), bias)
                reply(u, o[:HALF], lse[:HALF])
                o_loc[h] = o[HALF:]
                s_loc[h] = jnp.broadcast_to(lse[HALF:], (2 * T, D))

        @pl.when(ends)
        def _():
            for u in range(QG):
                h = g * QG + u
                q, bias = qf[pl.ds(HALF, HALF), wide(h)], bias_f[pl.ds(HALF, HALF), :]
                reply(u, *attend(q, *near(h), bias))

        @pl.when(has_right)
        def _():
            lse_copy(1, g).start()

        return 0

    lax.fori_loop(0, ng, step_f1, 0)

    def step_f0(g, _):
        @pl.when(prompt)
        def _():
            q_next(AHEAD + 2 * ng + g)

        @pl.when(has_right)
        def _():
            q_arrived(2, g)

        @pl.when(has_left)
        def _():
            for u in range(QG):
                arrived(l_recv.at[1, g * QG + u], l_rs.at[1, g * QG + u])

        kv = kv_row > 0.5
        for u in range(QG):
            h = g * QG + u
            low, got = l_recv[1, h], m_recv[h]
            keys = jnp.concatenate(
                [low[:PART], got[:MID], ek[:, wide(h)], k2[:, wide(h)]], axis=0
            )
            vals = jnp.concatenate(
                [low[PART:], got[MID:], ev[:, wide(h)], v2[:, wide(h)]], axis=0
            )
            o, lse = attend(qf[pl.ds(0, HALF), wide(h)], keys, vals, bias_f[pl.ds(0, HALF), :])
            lse_send[2, g, pl.ds(u, 1), :] = jnp.where(
                kv | (lane >= HALF), HIDDEN, to_row(lse, eyes[0])
            )
            rows = pl.ds(T - PART, PART)
            there = jnp.concatenate([k2[rows, wide(h)], v2[rows, wide(h)]], axis=0)
            l_send[0, h] = jnp.where(kv, there.astype(F32), o).astype(BF16)

            @pl.when(has_right)
            def _():
                l_copy(0, h).start()

        @pl.when(has_right)
        def _():
            lse_copy(2, g).start()

        return 0

    lax.fori_loop(0, ng, step_f0, 0)

    @pl.when(ends)
    def _():
        def step_own(g, _):
            for u in range(QG):
                own(g * QG + u, *near(g * QG + u))
            return 0

        lax.fori_loop(0, ng, step_own, 0)

    def put(g, side, act):
        cols = pl.ds(g * OG * D, OG * D)
        to = pl.ds(pl.multiple_of(core * w + g * OG * D, D), OG * D)
        src, dst, sem = stage.at[side, :, cols], out_ref.at[:, to], oo_ss.at[side, g]

        @pl.when(core == side)
        def _():
            act(pltpu.make_async_copy(src, dst, sem), False)

        @pl.when(core != side)
        def _():
            act(remote(src, dst, sem, oo_rs.at[g], sib), True)

    def begin(cp, far):
        cp.start()

    def sent(cp, far):
        if far:
            cp.wait_send()
        else:
            cp.wait()

    @pl.when(has_left)
    def _():
        for i in range(2):
            for g in range(ng):
                arrived(lse_recv.at[i, g], lse_rs.at[i, g])

    def finish_heads(i, g):
        step = g * (OG // QG) + i

        @pl.when(has_left)
        def _():
            arrived(lse_recv.at[2, step], lse_rs.at[2, step])
            for u in range(QG):
                h = step * QG + u
                arrived(l_recv.at[0, h], l_rs.at[0, h])

        for u in range(QG):
            h = step * QG + u
            low, mid = l_recv[0, h], l_recv[1, h]
            keys = jnp.concatenate([low[:PART], mid[:PART]], axis=0)
            vals = jnp.concatenate([low[PART:], mid[PART:]], axis=0)
            theirs = jnp.concatenate([low, mid, m_recv[h], jnp.zeros((T - G, D), BF16)], axis=0)
            f_lse = jnp.maximum(
                lse_recv[1, step, pl.ds(u, 1), :], lse_recv[2, step, pl.ds(u, 1), :]
            )
            there = jnp.concatenate(
                [to_column(f_lse, eye), to_column(lse_recv[0, step, pl.ds(u, 1), :], eye)], axis=0
            )
            here = s_loc[h]
            s = scores(q2[:, wide(h)], keys, bias_a[...]) * C2
            top = jnp.maximum(jnp.max(s, axis=1, keepdims=True), there)
            top = jnp.maximum(here, top)
            p = jnp.exp2(s - top[:, :HALF])
            fade = jnp.exp2(here - top)
            extra = jnp.exp2(there - top)
            total = fade + extra + jnp.sum(p, axis=1, keepdims=True)
            out = o_loc[h] * fade + weigh(p, vals) + theirs.astype(F32) * extra
            out = (out / total).astype(BF16)
            lse = (top + jnp.log2(total)) * LN2
            for side in range(2):
                rows = slice(side * T, side * T + T)
                stage[side, :, wide(h)] = out[rows]
                sums[side, pl.ds(h, 1), :] = to_row(lse[rows], eye)
        return g

    for g in range(no):
        lax.fori_loop(0, OG // QG, finish_heads, g)
        put(g, 0, begin)
        put(g, 1, begin)

    own_sum = pltpu.make_async_copy(sums.at[core], sum_ref.at[core], sum_ss.at[0])
    far_sum = remote(sums.at[other], sum_ref.at[core], sum_ss.at[1], sum_rs, sib)
    own_sum.start()
    far_sum.start()

    id_sib.wait_send()
    for cp in sib_sends:
        cp.wait_send()

    @pl.when(has_right)
    def _():
        for cp in id_right:
            cp.wait_send()

        e_copy(0).wait_send()
        e_copy(1).wait_send()

        def drain(h, _):
            m_copy(h).wait_send()
            l_copy(1, h).wait_send()
            l_copy(0, h).wait_send()
            return 0

        lax.fori_loop(0, nh, drain, 0)
        for i in range(3):
            for g in range(ng):
                lse_copy(i, g).wait_send()

    @pl.when(has_left)
    def _():
        for cp in id_left:
            cp.wait_send()
        for i in range(3 * ng):

            @pl.when(prompt | (i >= PUMP - TWO))
            def _():
                q_copy(i // ng, i % ng).wait_send()

    for g in range(no):
        put(g, 0, sent)
        put(g, 1, sent)
        to = pl.ds(pl.multiple_of(other * w + g * OG * D, D), OG * D)
        arrived(out_ref.at[:, to], oo_rs.at[g])
    own_sum.wait()
    far_sum.wait_send()
    arrived(sum_ref.at[other], sum_rs)


CHUNKS = 8


def finish(nh, out_in, sum_in, out_ref, sum_ref, sem):
    size = out_in.shape[0] // CHUNKS
    cps = [
        pltpu.make_async_copy(
            out_in.at[pl.ds(i * size, size), :], out_ref.at[pl.ds(i * size, size), :], sem.at[i]
        )
        for i in range(CHUNKS)
    ]
    for cp in cps:
        cp.start()
    for i in range(2):
        sum_ref[pl.ds(i * nh, nh), :] = sum_in[i, pl.ds(0, nh), :]
    for cp in cps:
        cp.wait()


def shards(mesh, queries, keys, values, segment_ids):
    n, ncp = mesh.size, mesh.shape["cp"]
    width = queries.shape[1]
    heads = width // D
    nh = heads // 2
    ng, no = nh // QG, nh // OG
    w = nh * D
    pad = -(-nh // 8) * 8
    dma = pltpu.SemaphoreType.DMA
    scratch = [
        pltpu.VMEM((6, 1, T), jnp.int32),
        pltpu.VMEM((2 * T, w), BF16),
        pltpu.VMEM((2 * T, w), BF16),
        pltpu.VMEM((2 * T, w), BF16),
        pltpu.VMEM((G, w), BF16),
        pltpu.VMEM((T, w), BF16),
        pltpu.VMEM((END, w), BF16),
        pltpu.VMEM((END, w), BF16),
        pltpu.VMEM((nh, G, D), BF16),
        pltpu.VMEM((nh, G, D), BF16),
        pltpu.VMEM((2, nh, HALF, D), BF16),
        pltpu.VMEM((2, nh, HALF, D), BF16),
        pltpu.VMEM((3, ng, 8, T), F32),
        pltpu.VMEM((3, ng, 8, T), F32),
        pltpu.VMEM((G, 2 * T), F32),
        pltpu.VMEM((T, 3 * T), F32),
        pltpu.VMEM((2 * T, 3 * T), F32),
        pltpu.VMEM((2 * T, HALF), F32),
        pltpu.VMEM((nh, 2 * T, D), F32),
        pltpu.VMEM((nh, 2 * T, D), F32),
        pltpu.VMEM((2, T, w), BF16),
        pltpu.VMEM((2, pad, T), F32),
        pltpu.SemaphoreType.REGULAR,
        dma((5,)),
        dma((6,)),
        dma((4,)),
        dma((3,)),
        dma((3,)),
        dma((2,)),
        dma((2,)),
        dma((3, ng)),
        dma((3, ng)),
        dma((nh,)),
        dma((nh,)),
        dma((2, nh)),
        dma((2, nh)),
        dma((3, ng)),
        dma((3, ng)),
        dma((2, no)),
        dma((no,)),
        dma((2,)),
        dma,
    ]
    anywhere = pl.BlockSpec(memory_space=pl.ANY)
    vmem = pl.BlockSpec(memory_space=pltpu.VMEM)
    out, sums = pl.pallas_call(
        functools.partial(kernel, n, ncp, nh),
        out_shape=(
            jax.ShapeDtypeStruct((T, width), BF16),
            jax.ShapeDtypeStruct((2, pad, T), F32),
        ),
        in_specs=[anywhere, anywhere, anywhere, anywhere],
        out_specs=(anywhere, anywhere),
        scratch_shapes=scratch,
        compiler_params=pltpu.CompilerParams(
            collective_id=0, has_side_effects=True, vmem_limit_bytes=53 * 2**20
        ),
        cost_estimate=pl.CostEstimate(
            flops=heads * T * T * D * 20, bytes_accessed=8 * T * width, transcendentals=0
        ),
    )(queries, keys, values, segment_ids.reshape(1, T))
    return pl.pallas_call(
        functools.partial(finish, nh),
        out_shape=(
            jax.ShapeDtypeStruct((T, width), BF16),
            jax.ShapeDtypeStruct((heads, T), F32),
        ),
        in_specs=[anywhere, vmem],
        out_specs=(anywhere, vmem),
        scratch_shapes=[dma((CHUNKS,))],
        compiler_params=pltpu.CompilerParams(vmem_limit_bytes=48 * 2**20),
    )(out, sums)


def solution(mesh):
    both = ("grp", "cp")
    return jax.shard_map(
        functools.partial(shards, mesh),
        mesh=mesh,
        in_specs=(P(both, None), P(both, None), P(both, None), P(both)),
        out_specs=(P(both, None), P(None, both)),
        check_vma=False,
    )
```

```python
import functools
import math

import jax
import jax.numpy as jnp
from jax import lax
from jax.experimental import pallas as pl
from jax.experimental.pallas import tpu as pltpu
from jax.sharding import PartitionSpec as P

T = 128
HALF = T // 2
PART = T // 4
G = 96
MID = G // 2
END = T - PART - MID
D = 128
HIDDEN = -1e30
C2 = 1.0 / math.sqrt(D) / math.log(2.0)
LN2 = math.log(2.0)
MESH = pl.DeviceIdType.MESH
F32 = jnp.float32
BF16 = jnp.bfloat16

QG = 2
OG = 4
LINE = 16
AHEAD = 6
TWO = 2
PUMP = 18
MORE = 2
LINE = 16


def wide(h):
    return pl.ds(pl.multiple_of(h * D, D), D)


def scores(q, k, bias):
    return lax.dot_general(q, k, (((1,), (1,)), ((), ())), preferred_element_type=F32) + bias


def weigh(p, v):
    return lax.dot_general(
        p.astype(BF16), v, (((1,), (0,)), ((), ())), preferred_element_type=F32
    )


def attend(q, k, v, bias):
    s = scores(q, k, bias)
    top = jnp.max(s, axis=1, keepdims=True)
    p = jnp.exp2((s - top) * C2)
    total = jnp.sum(p, axis=1, keepdims=True)
    return weigh(p, v) * (1.0 / total), top * C2 + jnp.log2(total)


def kernel(
    n,
    ncp,
    nh,
    q_ref,
    k_ref,
    v_ref,
    id_ref,
    out_ref,
    sum_ref,
    ids,
    q2,
    k2,
    v2,
    qg,
    qf,
    ek,
    ev,
    m_send,
    m_recv,
    l_send,
    l_recv,
    lse_send,
    lse_recv,
    bias_r,
    bias_o,
    bias_a,
    for_me,
    o_loc,
    s_loc,
    stage,
    sums,
    go,
    id_ss,
    id_rs,
    lo_s,
    sib_ss,
    sib_rs,
    e_ss,
    e_rs,
    q_ss,
    q_rs,
    m_ss,
    m_rs,
    l_ss,
    l_rs,
    lse_ss,
    lse_rs,
    oo_ss,
    oo_rs,
    sum_ss,
    sum_rs,
):
    w = nh * D
    ng = nh // QG
    no = nh // OG
    me = lax.axis_index("grp") * ncp + lax.axis_index("cp")
    core = lax.rem(me, 2)
    first = me - core
    other = 1 - core
    has_left = first > 0
    has_right = first < n - 2
    waits = lax.rem(first, LINE) == 0
    prompt = jnp.logical_not(waits)
    ends = lax.rem(first, LINE) == LINE - 2
    lead = jnp.where(ends, PUMP, jnp.where(waits, TWO, AHEAD))

    def at(i):
        i = lax.rem(i + n, n)
        return (i // ncp, lax.rem(i, ncp))

    sib = at(first + other)
    right = [at(first + 2), at(first + 3)]
    left = [at(first - 2), at(first - 1)]
    ahead = at(me + 2)
    behind_me = at(me - 2)

    def remote(src, dst, ss, rs, to):
        return pltpu.make_async_remote_copy(
            src_ref=src, dst_ref=dst, send_sem=ss, recv_sem=rs, device_id=to, device_id_type=MESH
        )

    def greet(sem, to):
        pl.semaphore_signal(sem, inc=1, device_id=to, device_id_type=MESH)

    def arrived(dst, rs):
        remote(dst, dst, sum_ss.at[0], rs, sib).wait_recv()

    barrier = pltpu.get_barrier_semaphore()
    greet(barrier, sib)

    @pl.when(has_left)
    def _():
        greet(barrier, left[0])
        greet(barrier, left[1])

    mine = pl.ds(pl.multiple_of(core * w, D), w)
    its = pl.ds(pl.multiple_of(other * w, D), w)
    my_rows = pl.ds(pl.multiple_of(core * T, T), T)
    its_rows = pl.ds(pl.multiple_of(other * T, T), T)
    trio = ((k_ref, k2), (v_ref, v2), (q_ref, q2))
    local = [
        pltpu.make_async_copy(a.at[:, mine], b.at[my_rows, :], lo_s.at[i])
        for i, (a, b) in enumerate(trio)
    ]
    local.append(pltpu.make_async_copy(id_ref, ids.at[2 + core], lo_s.at[3]))
    for cp in local:
        cp.start()
    pl.semaphore_wait(barrier, 1 + 2 * has_right.astype(jnp.int32))

    @pl.when(has_right)
    def _():
        greet(go, right[0])
        greet(go, right[1])

    id_sib = remote(id_ref, ids.at[2 + core], id_ss.at[0], id_rs.at[2 + core], sib)
    id_right = [
        remote(id_ref, ids.at[core], id_ss.at[1 + i], id_rs.at[core], right[i]) for i in range(2)
    ]
    sib_sends = [
        remote(a.at[:, its], b.at[my_rows, :], sib_ss.at[i], sib_rs.at[i], sib)
        for i, (a, b) in enumerate(trio)
    ]

    def e_copies():
        return [
            remote(
                a.at[pl.ds(T - END, END), pl.ds(kk * w, w)],
                b,
                e_ss.at[kk, i],
                e_rs.at[i],
                right[kk],
            )
            for kk in range(2)
            for i, (a, b) in enumerate(((k_ref, ek), (v_ref, ev)))
        ]

    def q_cols(g):
        return pl.ds(pl.multiple_of(g * QG * D, D), QG * D)

    pieces = ((T, qg, 0, G), (HALF, qf, HALF, HALF), (0, qf, 0, HALF))

    def q_cut(piece, g):
        return wide(g) if piece == 0 else q_cols(g)

    def q_copy(piece, g):
        start, to, row, size = pieces[piece]
        return remote(
            q2.at[pl.ds(start, size), q_cut(piece, g)],
            to.at[pl.ds(row, size), q_cut(piece, g)],
            q_ss.at[piece, g],
            q_rs.at[piece, g],
            behind_me,
        )

    def q_arrived(piece, g):
        _, to, row, size = pieces[piece]
        arrived(to.at[pl.ds(row, size), q_cut(piece, g)], q_rs.at[piece, g])

    q_order = [(0, h) for h in range(nh)] + [(p, g) for p in (1, 2) for g in range(ng)]

    def q_next(i):
        for piece, start, count in ((0, 0, nh), (1, nh, ng), (2, nh + ng, ng)):

            @pl.when(has_left & (i >= start) & (i < start + count))
            def _():
                q_copy(piece, i - start).start()

    sib_sends[2].start()
    id_sib.start()
    sib_sends[0].start()
    sib_sends[1].start()

    @pl.when(has_right)
    def _():
        id_right[0].start()
        id_right[1].start()

        @pl.when(core == 1)
        def _():
            for cp in e_copies():
                cp.start()

    @pl.when(jnp.logical_not(has_left))
    def _():
        ids[0] = jnp.full((1, T), -1, jnp.int32)
        ids[1] = jnp.full((1, T), -1, jnp.int32)
        ek[...] = jnp.zeros(ek.shape, BF16)
        ev[...] = jnp.zeros(ev.shape, BF16)
        m_recv[...] = jnp.zeros(m_recv.shape, BF16)
        l_recv[...] = jnp.zeros(l_recv.shape, BF16)
        lse_recv[...] = jnp.full(lse_recv.shape, HIDDEN, F32)

    def iota(shape, axis):
        return lax.broadcasted_iota(jnp.int32, shape, axis)

    eye = iota((T, T), 0) == iota((T, T), 1)
    eyes = [iota((HALF, T), 0) + HALF * i == iota((HALF, T), 1) for i in range(2)]
    eye_g = iota((G, T), 0) == iota((G, T), 1)

    def to_column(r, like):
        return jnp.sum(
            jnp.where(like, jnp.broadcast_to(r, like.shape), 0.0), axis=1, keepdims=True
        )

    def to_row(x, like):
        return jnp.sum(jnp.where(like, x, 0.0), axis=0, keepdims=True)

    def bias_of(q_col, k_row):
        return jnp.where(q_col == k_row, 0.0, HIDDEN)

    def have(i):
        local[i].wait()
        arrived(trio[i][1].at[its_rows, :], sib_rs.at[i])

    have(0)
    have(1)

    have(2)
    arrived(ids.at[2 + other], id_rs.at[2 + other])
    local[3].wait()
    own = [ids[2].astype(F32), ids[3].astype(F32)]
    own_col = [to_column(r, eye) for r in own]
    for i in range(2):
        for j in range(2):
            bias_o[pl.ds(i * T, T), pl.ds((j + 1) * T, T)] = (
                bias_of(own_col[i], own[j]) if j <= i else jnp.full((T, T), HIDDEN, F32)
            )

    lane = iota((1, T), 1)

    def short(a, b):
        edge = jnp.sum(jnp.where(lane == T - PART - 1, a, 0.0), axis=1, keepdims=True)
        return edge != jnp.max(b, axis=1, keepdims=True)

    kv_row = jnp.broadcast_to(jnp.where(short(*own), 1.0, 0.0), (1, D))

    @pl.when(has_left)
    def _():
        pl.semaphore_wait(go, 2)
        for i in range(PUMP):

            @pl.when(i < lead)
            def _():
                q_copy(*q_order[i]).start()

    across = jnp.max(own[1], axis=1, keepdims=True)

    def bias_across(k_row):
        return jnp.where(k_row == across, 0.0, HIDDEN)

    for j in range(2):
        for i in range(2):
            bias_r[pl.ds(i, 1), pl.ds((j + 1) * T, T)] = bias_across(own[j])

    def m_copy(h):
        return remote(m_send.at[h], m_recv.at[h], m_ss.at[h], m_rs.at[h], ahead)

    def l_copy(part, h):
        return remote(
            l_send.at[part, h], l_recv.at[part, h], l_ss.at[part, h], l_rs.at[part, h], ahead
        )

    def lse_copy(i, g):
        return remote(
            lse_send.at[i, g], lse_recv.at[i, g], lse_ss.at[i, g], lse_rs.at[i, g], ahead
        )

    def step_g(h, _):
        q_next(lead + h)

        @pl.when(has_right)
        def _():
            q_arrived(0, h)

        kv = kv_row > 0.5
        g, u = h // QG, lax.rem(h, QG)
        o, lse = attend(
            qg[:, wide(h)], k2[:, wide(h)], v2[:, wide(h)], bias_r[pl.ds(0, 1), pl.ds(T, 2 * T)]
        )
        lse_send[0, g, pl.ds(u, 1), :] = jnp.where(kv | (lane >= G), HIDDEN, to_row(lse, eye_g))
        rows = pl.ds(T + PART, MID)
        there = jnp.concatenate([k2[rows, wide(h)], v2[rows, wide(h)]], axis=0)
        m_send[h] = jnp.where(kv, there.astype(F32), o).astype(BF16)

        @pl.when(has_right)
        def _():
            m_copy(h).start()

            @pl.when(u == QG - 1)
            def _():
                lse_copy(0, g).start()

        return 0

    lax.fori_loop(0, nh, step_g, 0)

    @pl.when(waits & has_left)
    def _():
        for i in range(TWO + nh, PUMP):
            q_copy(*q_order[i]).start()

    @pl.when(has_left)
    def _():
        arrived(ids.at[0], id_rs.at[0])
        arrived(ids.at[1], id_rs.at[1])
        arrived(ek, e_rs.at[0])
        arrived(ev, e_rs.at[1])

    before = [ids[i].astype(F32) for i in range(2)]
    seen = [jnp.where(short(*before), r, -1.0) for r in before]
    behind = seen[1]
    low_keys = jnp.concatenate([seen[0][:, T - PART :], behind[:, :PART]], axis=1)
    for i in range(2):
        rows = pl.ds(i * T, T)
        bias_o[rows, pl.ds(0, T)] = jnp.where(
            iota((T, T), 1) < PART, HIDDEN, bias_of(own_col[i], behind)
        )
        bias_a[rows, :] = bias_of(own_col[i], low_keys)
    bias_r[pl.ds(0, 1), pl.ds(0, T)] = jnp.where(lane < PART, HIDDEN, bias_across(behind))
    bias_r[pl.ds(1, 1), pl.ds(0, T)] = bias_across(behind)
    from_left = jnp.max(before[1], axis=1, keepdims=True)
    for i in range(2):
        for_me[pl.ds(i, 1), :] = jnp.where(own[i] == from_left, 0.0, 2.0 * HIDDEN)

    def near(h):
        none = jnp.zeros((PART, D), BF16)
        got = m_recv[h]
        keys = jnp.concatenate([none, got[:MID], ek[:, wide(h)], k2[:, wide(h)]], axis=0)
        vals = jnp.concatenate([none, got[MID:], ev[:, wide(h)], v2[:, wide(h)]], axis=0)
        return keys, vals

    def own(h, keys, vals):
        o_loc[h], lse = attend(q2[:, wide(h)], keys, vals, bias_o[...])
        s_loc[h] = jnp.broadcast_to(lse, (2 * T, D))

    def step_f1(g, _):
        @pl.when(waits)
        def _():
            for i in range(MORE):
                q_next(PUMP + g * MORE + i)

        @pl.when(prompt)
        def _():
            q_next(lead + nh + g)

        @pl.when(has_right)
        def _():
            q_arrived(1, g)

        @pl.when(has_left)
        def _():
            for u in range(QG):
                arrived(m_recv.at[g * QG + u], m_rs.at[g * QG + u])

        def reply(u, o, lse):
            h = g * QG + u
            kv = kv_row > 0.5
            lse_send[1, g, pl.ds(u, 1), :] = jnp.where(
                kv | (lane < HALF), HIDDEN, to_row(lse, eyes[1])
            )
            rows = pl.ds(T, PART)
            there = jnp.concatenate([k2[rows, wide(h)], v2[rows, wide(h)]], axis=0)
            l_send[1, h] = jnp.where(kv, there.astype(F32), o).astype(BF16)

            @pl.when(has_right)
            def _():
                l_copy(1, h).start()

        @pl.when(jnp.logical_not(ends))
        def _():
            for u in range(QG):
                h = g * QG + u
                q = jnp.concatenate([qf[pl.ds(HALF, HALF), wide(h)], q2[:, wide(h)]], axis=0)
                bias = jnp.concatenate(
                    [jnp.broadcast_to(bias_r[pl.ds(0, 1), :], (HALF, 3 * T)), bias_o[...]], axis=0
                )
                o, lse = attend(q, *near(h), bias)
                reply(u, o[:HALF], lse[:HALF])
                o_loc[h] = o[HALF:]
                s_loc[h] = jnp.broadcast_to(lse[HALF:], (2 * T, D))

        @pl.when(ends)
        def _():
            for u in range(QG):
                h = g * QG + u
                q, bias = qf[pl.ds(HALF, HALF), wide(h)], bias_r[pl.ds(0, 1), :]
                reply(u, *attend(q, *near(h), bias))

        @pl.when(has_right)
        def _():
            lse_copy(1, g).start()

        return 0

    lax.fori_loop(0, ng, step_f1, 0)

    def step_f0(g, _):
        @pl.when(prompt)
        def _():
            q_next(lead + nh + ng + g)

        @pl.when(has_right)
        def _():
            q_arrived(2, g)

        @pl.when(has_left)
        def _():
            for u in range(QG):
                arrived(l_recv.at[1, g * QG + u], l_rs.at[1, g * QG + u])

        kv = kv_row > 0.5
        for u in range(QG):
            h = g * QG + u
            low, got = l_recv[1, h], m_recv[h]
            keys = jnp.concatenate(
                [low[:PART], got[:MID], ek[:, wide(h)], k2[:, wide(h)]], axis=0
            )
            vals = jnp.concatenate(
                [low[PART:], got[MID:], ev[:, wide(h)], v2[:, wide(h)]], axis=0
            )
            o, lse = attend(qf[pl.ds(0, HALF), wide(h)], keys, vals, bias_r[pl.ds(1, 1), :])
            lse_send[2, g, pl.ds(u, 1), :] = jnp.where(
                kv | (lane >= HALF), HIDDEN, to_row(lse, eyes[0])
            )
            rows = pl.ds(T - PART, PART)
            there = jnp.concatenate([k2[rows, wide(h)], v2[rows, wide(h)]], axis=0)
            l_send[0, h] = jnp.where(kv, there.astype(F32), o).astype(BF16)

            @pl.when(has_right)
            def _():
                l_copy(0, h).start()

        @pl.when(has_right)
        def _():
            lse_copy(2, g).start()

        return 0

    lax.fori_loop(0, ng, step_f0, 0)

    @pl.when(ends)
    def _():
        def step_own(g, _):
            for u in range(QG):
                own(g * QG + u, *near(g * QG + u))
            return 0

        lax.fori_loop(0, ng, step_own, 0)

    def put(g, side, act):
        cols = pl.ds(g * OG * D, OG * D)
        to = pl.ds(pl.multiple_of(core * w + g * OG * D, D), OG * D)
        src, dst, sem = stage.at[side, :, cols], out_ref.at[:, to], oo_ss.at[side, g]

        @pl.when(core == side)
        def _():
            act(pltpu.make_async_copy(src, dst, sem), False)

        @pl.when(core != side)
        def _():
            act(remote(src, dst, sem, oo_rs.at[g], sib), True)

    def begin(cp, far):
        cp.start()

    def sent(cp, far):
        if far:
            cp.wait_send()
        else:
            cp.wait()

    @pl.when(has_left)
    def _():
        for i in range(2):
            for g in range(ng):
                arrived(lse_recv.at[i, g], lse_rs.at[i, g])

    def finish_heads(i, g):
        step = g * (OG // QG) + i

        @pl.when(has_left)
        def _():
            arrived(lse_recv.at[2, step], lse_rs.at[2, step])
            for u in range(QG):
                h = step * QG + u
                arrived(l_recv.at[0, h], l_rs.at[0, h])

        for u in range(QG):
            h = step * QG + u
            low, mid = l_recv[0, h], l_recv[1, h]
            keys = jnp.concatenate([low[:PART], mid[:PART]], axis=0)
            vals = jnp.concatenate([low[PART:], mid[PART:]], axis=0)
            theirs = jnp.concatenate([low, mid, m_recv[h], jnp.zeros((T - G, D), BF16)], axis=0)
            f_lse = jnp.maximum(
                lse_recv[1, step, pl.ds(u, 1), :], lse_recv[2, step, pl.ds(u, 1), :]
            )
            there = jnp.concatenate(
                [
                    to_column(f_lse + for_me[pl.ds(0, 1), :], eye),
                    to_column(lse_recv[0, step, pl.ds(u, 1), :] + for_me[pl.ds(1, 1), :], eye),
                ],
                axis=0,
            )
            here = s_loc[h]
            s = scores(q2[:, wide(h)], keys, bias_a[...]) * C2
            top = jnp.maximum(jnp.max(s, axis=1, keepdims=True), there)
            top = jnp.maximum(here, top)
            p = jnp.exp2(s - top[:, :HALF])
            fade = jnp.exp2(here - top)
            extra = jnp.exp2(there - top)
            total = fade + extra + jnp.sum(p, axis=1, keepdims=True)
            out = o_loc[h] * fade + weigh(p, vals) + theirs.astype(F32) * extra
            out = (out / total).astype(BF16)
            lse = (top + jnp.log2(total)) * LN2
            for side in range(2):
                rows = slice(side * T, side * T + T)
                stage[side, :, wide(h)] = out[rows]
                sums[side, pl.ds(h, 1), :] = to_row(lse[rows], eye)
        return g

    def drained():
        id_sib.wait_send()
        for cp in sib_sends:
            cp.wait_send()

        @pl.when(has_right)
        def _():
            for cp in id_right:
                cp.wait_send()

            @pl.when(core == 1)
            def _():
                for cp in e_copies():
                    cp.wait_send()

            def drain(h, _):
                m_copy(h).wait_send()
                l_copy(1, h).wait_send()
                l_copy(0, h).wait_send()
                return 0

            lax.fori_loop(0, nh, drain, 0)
            for i in range(3):
                for g in range(ng):
                    lse_copy(i, g).wait_send()

        @pl.when(has_left)
        def _():
            for q in q_order:
                q_copy(*q).wait_send()

    for g in range(no):
        lax.fori_loop(0, OG // QG, finish_heads, g)
        put(g, 0, begin)
        put(g, 1, begin)

    own_sum = pltpu.make_async_copy(sums.at[core], sum_ref.at[core], sum_ss.at[0])
    far_sum = remote(sums.at[other], sum_ref.at[core], sum_ss.at[1], sum_rs, sib)
    own_sum.start()
    far_sum.start()
    drained()

    for g in range(no):
        put(g, 0, sent)
        put(g, 1, sent)
        to = pl.ds(pl.multiple_of(other * w + g * OG * D, D), OG * D)
        arrived(out_ref.at[:, to], oo_rs.at[g])
    own_sum.wait()
    far_sum.wait_send()
    arrived(sum_ref.at[other], sum_rs)


CHUNKS = 4


def finish(nh, out_in, sum_in, out_ref, sum_ref, hold, sem):
    size = out_in.shape[0] // CHUNKS
    cps = [
        pltpu.make_async_copy(
            out_in.at[pl.ds(i * size, size), :], out_ref.at[pl.ds(i * size, size), :], sem.at[i]
        )
        for i in range(CHUNKS)
    ]
    cps.append(pltpu.make_async_copy(hold, sum_ref, sem.at[CHUNKS]))
    for cp in cps[:-1]:
        cp.start()
    for i in range(2):
        hold[pl.ds(i * nh, nh), :] = sum_in[i, pl.ds(0, nh), :]
    cps[-1].start()
    for cp in cps:
        cp.wait()


def shards(mesh, queries, keys, values, segment_ids):
    n, ncp = mesh.size, mesh.shape["cp"]
    width = queries.shape[1]
    heads = width // D
    nh = heads // 2
    ng, no = nh // QG, nh // OG
    w = nh * D
    pad = -(-nh // 8) * 8
    dma = pltpu.SemaphoreType.DMA
    scratch = [
        pltpu.VMEM((4, 1, T), jnp.int32),
        pltpu.VMEM((2 * T, w), BF16),
        pltpu.VMEM((2 * T, w), BF16),
        pltpu.VMEM((2 * T, w), BF16),
        pltpu.VMEM((G, w), BF16),
        pltpu.VMEM((T, w), BF16),
        pltpu.VMEM((END, w), BF16),
        pltpu.VMEM((END, w), BF16),
        pltpu.VMEM((nh, G, D), BF16),
        pltpu.VMEM((nh, G, D), BF16),
        pltpu.VMEM((2, nh, HALF, D), BF16),
        pltpu.VMEM((2, nh, HALF, D), BF16),
        pltpu.VMEM((3, ng, 8, T), F32),
        pltpu.VMEM((3, ng, 8, T), F32),
        pltpu.VMEM((8, 3 * T), F32),
        pltpu.VMEM((2 * T, 3 * T), F32),
        pltpu.VMEM((2 * T, HALF), F32),
        pltpu.VMEM((8, T), F32),
        pltpu.VMEM((nh, 2 * T, D), F32),
        pltpu.VMEM((nh, 2 * T, D), F32),
        pltpu.VMEM((2, T, w), BF16),
        pltpu.VMEM((2, pad, T), F32),
        pltpu.SemaphoreType.REGULAR,
        dma((3,)),
        dma((4,)),
        dma((4,)),
        dma((3,)),
        dma((3,)),
        dma((2, 2)),
        dma((2,)),
        dma((3, nh)),
        dma((3, nh)),
        dma((nh,)),
        dma((nh,)),
        dma((2, nh)),
        dma((2, nh)),
        dma((3, ng)),
        dma((3, ng)),
        dma((2, no)),
        dma((no,)),
        dma((2,)),
        dma,
    ]
    anywhere = pl.BlockSpec(memory_space=pl.ANY)
    vmem = pl.BlockSpec(memory_space=pltpu.VMEM)
    operands = (queries, keys, values, segment_ids.reshape(1, T))
    out, sums = pl.pallas_call(
        functools.partial(kernel, n, ncp, nh),
        out_shape=(
            jax.ShapeDtypeStruct((T, width), BF16),
            jax.ShapeDtypeStruct((2, pad, T), F32),
        ),
        in_specs=[anywhere, anywhere, anywhere, anywhere],
        out_specs=(anywhere, anywhere),
        scratch_shapes=scratch,
        compiler_params=pltpu.CompilerParams(
            collective_id=0, has_side_effects=True, vmem_limit_bytes=48 * 2**20
        ),
        cost_estimate=pl.CostEstimate(
            flops=heads * T * T * D * 20, bytes_accessed=8 * T * width, transcendentals=0
        ),
    )(*[pltpu.with_memory_space_constraint(a, pltpu.HBM) for a in operands])
    return pl.pallas_call(
        functools.partial(finish, nh),
        out_shape=(
            jax.ShapeDtypeStruct((T, width), BF16),
            jax.ShapeDtypeStruct((heads, T), F32),
        ),
        in_specs=[anywhere, vmem],
        out_specs=(anywhere, anywhere),
        scratch_shapes=[pltpu.VMEM((heads, T), F32), dma((CHUNKS + 1,))],
        compiler_params=pltpu.CompilerParams(vmem_limit_bytes=48 * 2**20),
    )(out, sums)


def solution(mesh):
    both = ("grp", "cp")
    return jax.shard_map(
        functools.partial(shards, mesh),
        mesh=mesh,
        in_specs=(P(both, None), P(both, None), P(both, None), P(both)),
        out_specs=(P(both, None), P(None, both)),
        check_vma=False,
    )
```

```python
import functools
import math

import jax
import jax.numpy as jnp
from jax import lax
from jax.experimental import pallas as pl
from jax.experimental.pallas import tpu as pltpu
from jax.sharding import PartitionSpec as P

T = 128
HALF = T // 2
PART = T // 4
G = 96
MID = G // 2
END = T - PART - MID
D = 128
HIDDEN = -1e30
C2 = 1.0 / math.sqrt(D) / math.log(2.0)
LN2 = math.log(2.0)
MESH = pl.DeviceIdType.MESH
F32 = jnp.float32
BF16 = jnp.bfloat16

QG = 2
OG = 2
LINE = 16
AHEAD = 6
TWO = 2
PUMP = 18
MORE = 2
LINE = 16


def wide(h):
    return pl.ds(pl.multiple_of(h * D, D), D)


def scores(q, k, bias):
    return lax.dot_general(q, k, (((1,), (1,)), ((), ())), preferred_element_type=F32) + bias


def weigh(p, v):
    return lax.dot_general(
        p.astype(BF16), v, (((1,), (0,)), ((), ())), preferred_element_type=F32
    )


def attend(q, k, v, bias):
    s = scores(q, k, bias)
    top = jnp.max(s, axis=1, keepdims=True)
    p = jnp.exp2((s - top) * C2)
    total = jnp.sum(p, axis=1, keepdims=True)
    return weigh(p, v) * (1.0 / total), top * C2 + jnp.log2(total)


def kernel(
    n,
    ncp,
    nh,
    q_ref,
    k_ref,
    v_ref,
    id_ref,
    out_ref,
    sum_ref,
    ids,
    q2,
    k2,
    v2,
    qg,
    qf,
    ek,
    ev,
    m_send,
    m_recv,
    l_send,
    l_recv,
    lse_send,
    lse_recv,
    bias_r,
    bias_o,
    bias_a,
    for_me,
    l_col,
    o_loc,
    s_loc,
    stage,
    sums,
    go,
    id_ss,
    id_rs,
    lo_s,
    sib_ss,
    sib_rs,
    e_ss,
    e_rs,
    q_ss,
    q_rs,
    m_ss,
    m_rs,
    l_ss,
    l_rs,
    lse_ss,
    lse_rs,
    oo_ss,
    oo_rs,
    sum_ss,
    sum_rs,
):
    w = nh * D
    ng = nh // QG
    no = nh // OG
    me = lax.axis_index("grp") * ncp + lax.axis_index("cp")
    core = lax.rem(me, 2)
    first = me - core
    other = 1 - core
    has_left = first > 0
    has_right = first < n - 2
    waits = lax.rem(first, LINE) == 0
    prompt = jnp.logical_not(waits)
    ends = lax.rem(first, LINE) == LINE - 2
    lead = jnp.where(ends, PUMP, jnp.where(waits, TWO, AHEAD))

    def at(i):
        i = lax.rem(i + n, n)
        return (i // ncp, lax.rem(i, ncp))

    sib = at(first + other)
    right = [at(first + 2), at(first + 3)]
    left = [at(first - 2), at(first - 1)]
    ahead = at(me + 2)
    behind_me = at(me - 2)

    def remote(src, dst, ss, rs, to):
        return pltpu.make_async_remote_copy(
            src_ref=src, dst_ref=dst, send_sem=ss, recv_sem=rs, device_id=to, device_id_type=MESH
        )

    def greet(sem, to):
        pl.semaphore_signal(sem, inc=1, device_id=to, device_id_type=MESH)

    def arrived(dst, rs):
        remote(dst, dst, sum_ss.at[0], rs, sib).wait_recv()

    barrier = pltpu.get_barrier_semaphore()
    greet(barrier, sib)

    @pl.when(has_left)
    def _():
        greet(barrier, left[0])
        greet(barrier, left[1])

    mine = pl.ds(pl.multiple_of(core * w, D), w)
    its = pl.ds(pl.multiple_of(other * w, D), w)
    my_rows = pl.ds(pl.multiple_of(core * T, T), T)
    its_rows = pl.ds(pl.multiple_of(other * T, T), T)
    trio = ((k_ref, k2), (v_ref, v2), (q_ref, q2))
    local = [
        pltpu.make_async_copy(a.at[:, mine], b.at[my_rows, :], lo_s.at[i])
        for i, (a, b) in enumerate(trio)
    ]
    local.append(pltpu.make_async_copy(id_ref, ids.at[2 + core], lo_s.at[3]))
    for cp in local:
        cp.start()
    pl.semaphore_wait(barrier, 1 + 2 * has_right.astype(jnp.int32))

    @pl.when(has_right)
    def _():
        greet(go, right[0])
        greet(go, right[1])

    id_sib = remote(id_ref, ids.at[2 + core], id_ss.at[0], id_rs.at[2 + core], sib)
    id_right = [
        remote(id_ref, ids.at[core], id_ss.at[1 + i], id_rs.at[core], right[i]) for i in range(2)
    ]
    sib_sends = [
        remote(a.at[:, its], b.at[my_rows, :], sib_ss.at[i], sib_rs.at[i], sib)
        for i, (a, b) in enumerate(trio)
    ]

    def e_copies():
        return [
            remote(
                a.at[pl.ds(T - END, END), pl.ds(kk * w, w)],
                b,
                e_ss.at[kk, i],
                e_rs.at[i],
                right[kk],
            )
            for kk in range(2)
            for i, (a, b) in enumerate(((k_ref, ek), (v_ref, ev)))
        ]

    def q_cols(g):
        return pl.ds(pl.multiple_of(g * QG * D, D), QG * D)

    pieces = ((T, qg, 0, G), (HALF, qf, HALF, HALF), (0, qf, 0, HALF))

    def q_cut(piece, g):
        return wide(g) if piece == 0 else q_cols(g)

    def q_copy(piece, g):
        start, to, row, size = pieces[piece]
        return remote(
            q2.at[pl.ds(start, size), q_cut(piece, g)],
            to.at[pl.ds(row, size), q_cut(piece, g)],
            q_ss.at[piece, g],
            q_rs.at[piece, g],
            behind_me,
        )

    def q_arrived(piece, g):
        _, to, row, size = pieces[piece]
        arrived(to.at[pl.ds(row, size), q_cut(piece, g)], q_rs.at[piece, g])

    q_order = [(0, h) for h in range(nh)] + [(p, g) for p in (1, 2) for g in range(ng)]

    def q_next(i):
        for piece, start, count in ((0, 0, nh), (1, nh, ng), (2, nh + ng, ng)):

            @pl.when(has_left & (i >= start) & (i < start + count))
            def _():
                q_copy(piece, i - start).start()

    sib_sends[2].start()
    id_sib.start()
    sib_sends[0].start()
    sib_sends[1].start()

    @pl.when(has_right)
    def _():
        id_right[0].start()
        id_right[1].start()

        @pl.when(core == 1)
        def _():
            for cp in e_copies():
                cp.start()

    @pl.when(jnp.logical_not(has_left))
    def _():
        ids[0] = jnp.full((1, T), -1, jnp.int32)
        ids[1] = jnp.full((1, T), -1, jnp.int32)
        ek[...] = jnp.zeros(ek.shape, BF16)
        ev[...] = jnp.zeros(ev.shape, BF16)
        m_recv[...] = jnp.zeros(m_recv.shape, BF16)
        l_recv[...] = jnp.zeros(l_recv.shape, BF16)
        lse_recv[...] = jnp.full(lse_recv.shape, HIDDEN, F32)

    def iota(shape, axis):
        return lax.broadcasted_iota(jnp.int32, shape, axis)

    eye = iota((T, T), 0) == iota((T, T), 1)
    eyes = [iota((HALF, T), 0) + HALF * i == iota((HALF, T), 1) for i in range(2)]
    eye_g = iota((G, T), 0) == iota((G, T), 1)

    def to_column(r, like):
        return jnp.sum(
            jnp.where(like, jnp.broadcast_to(r, like.shape), 0.0), axis=1, keepdims=True
        )

    def to_row(x, like):
        return jnp.sum(jnp.where(like, x, 0.0), axis=0, keepdims=True)

    def bias_of(q_col, k_row):
        return jnp.where(q_col == k_row, 0.0, HIDDEN)

    def have(i):
        local[i].wait()
        arrived(trio[i][1].at[its_rows, :], sib_rs.at[i])

    have(0)
    have(1)

    have(2)
    arrived(ids.at[2 + other], id_rs.at[2 + other])
    local[3].wait()
    own = [ids[2].astype(F32), ids[3].astype(F32)]
    own_col = [to_column(r, eye) for r in own]
    for i in range(2):
        for j in range(2):
            bias_o[pl.ds(i * T, T), pl.ds((j + 1) * T, T)] = (
                bias_of(own_col[i], own[j]) if j <= i else jnp.full((T, T), HIDDEN, F32)
            )

    lane = iota((1, T), 1)

    def short(a, b):
        edge = jnp.sum(jnp.where(lane == T - PART - 1, a, 0.0), axis=1, keepdims=True)
        return edge != jnp.max(b, axis=1, keepdims=True)

    kv_row = jnp.broadcast_to(jnp.where(short(*own), 1.0, 0.0), (1, D))

    @pl.when(has_left)
    def _():
        pl.semaphore_wait(go, 2)
        for i in range(PUMP):

            @pl.when(i < lead)
            def _():
                q_copy(*q_order[i]).start()

    across = jnp.max(own[1], axis=1, keepdims=True)

    def bias_across(k_row):
        return jnp.where(k_row == across, 0.0, HIDDEN)

    for j in range(2):
        for i in range(2):
            bias_r[pl.ds(i, 1), pl.ds((j + 1) * T, T)] = bias_across(own[j])

    def m_copy(h):
        return remote(m_send.at[h], m_recv.at[h], m_ss.at[h], m_rs.at[h], ahead)

    def l_copy(part, h):
        return remote(
            l_send.at[part, h], l_recv.at[part, h], l_ss.at[part, h], l_rs.at[part, h], ahead
        )

    def lse_copy(i, g):
        return remote(
            lse_send.at[i, g], lse_recv.at[i, g], lse_ss.at[i, g], lse_rs.at[i, g], ahead
        )

    def step_g(h, _):
        q_next(lead + h)

        @pl.when(has_right)
        def _():
            q_arrived(0, h)

        kv = kv_row > 0.5
        g, u = h // QG, lax.rem(h, QG)
        o, lse = attend(
            qg[:, wide(h)], k2[:, wide(h)], v2[:, wide(h)], bias_r[pl.ds(0, 1), pl.ds(T, 2 * T)]
        )
        lse_send[0, g, pl.ds(u, 1), :] = jnp.where(kv | (lane >= G), HIDDEN, to_row(lse, eye_g))
        rows = pl.ds(T + PART, MID)
        there = jnp.concatenate([k2[rows, wide(h)], v2[rows, wide(h)]], axis=0)
        m_send[h] = jnp.where(kv, there.astype(F32), o).astype(BF16)

        @pl.when(has_right)
        def _():
            m_copy(h).start()

            @pl.when(u == QG - 1)
            def _():
                lse_copy(0, g).start()

        return 0

    lax.fori_loop(0, nh, step_g, 0)

    @pl.when(waits & has_left)
    def _():
        for i in range(TWO + nh, PUMP):
            q_copy(*q_order[i]).start()

    @pl.when(has_left)
    def _():
        arrived(ids.at[0], id_rs.at[0])
        arrived(ids.at[1], id_rs.at[1])
        arrived(ek, e_rs.at[0])
        arrived(ev, e_rs.at[1])

    before = [ids[i].astype(F32) for i in range(2)]
    seen = [jnp.where(short(*before), r, -1.0) for r in before]
    behind = seen[1]
    low_keys = jnp.concatenate([seen[0][:, T - PART :], behind[:, :PART]], axis=1)
    for i in range(2):
        rows = pl.ds(i * T, T)
        bias_o[rows, pl.ds(0, T)] = jnp.where(
            iota((T, T), 1) < PART, HIDDEN, bias_of(own_col[i], behind)
        )
        bias_a[rows, :] = bias_of(own_col[i], low_keys)
    bias_r[pl.ds(0, 1), pl.ds(0, T)] = jnp.where(lane < PART, HIDDEN, bias_across(behind))
    bias_r[pl.ds(1, 1), pl.ds(0, T)] = bias_across(behind)
    from_left = jnp.max(before[1], axis=1, keepdims=True)
    for i in range(2):
        for_me[pl.ds(i, 1), :] = jnp.where(own[i] == from_left, 0.0, 2.0 * HIDDEN)

    def near(h):
        none = jnp.zeros((PART, D), BF16)
        got = m_recv[h]
        keys = jnp.concatenate([none, got[:MID], ek[:, wide(h)], k2[:, wide(h)]], axis=0)
        vals = jnp.concatenate([none, got[MID:], ev[:, wide(h)], v2[:, wide(h)]], axis=0)
        return keys, vals

    def own(h, keys, vals):
        o_loc[h], lse = attend(q2[:, wide(h)], keys, vals, bias_o[...])
        s_loc[h] = jnp.broadcast_to(lse, (2 * T, D))

    def step_f1(g, _):
        @pl.when(waits)
        def _():
            for i in range(MORE):
                q_next(PUMP + g * MORE + i)

        @pl.when(prompt)
        def _():
            q_next(lead + nh + g)

        @pl.when(has_right)
        def _():
            q_arrived(1, g)

        @pl.when(has_left)
        def _():
            for u in range(QG):
                arrived(m_recv.at[g * QG + u], m_rs.at[g * QG + u])

        def reply(u, o, lse):
            h = g * QG + u
            kv = kv_row > 0.5
            lse_send[1, g, pl.ds(u, 1), :] = jnp.where(
                kv | (lane < HALF), HIDDEN, to_row(lse, eyes[1])
            )
            rows = pl.ds(T, PART)
            there = jnp.concatenate([k2[rows, wide(h)], v2[rows, wide(h)]], axis=0)
            l_send[1, h] = jnp.where(kv, there.astype(F32), o).astype(BF16)

            @pl.when(has_right)
            def _():
                l_copy(1, h).start()

        @pl.when(jnp.logical_not(ends))
        def _():
            for u in range(QG):
                h = g * QG + u
                q = jnp.concatenate([qf[pl.ds(HALF, HALF), wide(h)], q2[:, wide(h)]], axis=0)
                bias = jnp.concatenate(
                    [jnp.broadcast_to(bias_r[pl.ds(0, 1), :], (HALF, 3 * T)), bias_o[...]], axis=0
                )
                o, lse = attend(q, *near(h), bias)
                reply(u, o[:HALF], lse[:HALF])
                o_loc[h] = o[HALF:]
                s_loc[h] = jnp.broadcast_to(lse[HALF:], (2 * T, D))

        @pl.when(ends)
        def _():
            for u in range(QG):
                h = g * QG + u
                q, bias = qf[pl.ds(HALF, HALF), wide(h)], bias_r[pl.ds(0, 1), :]
                reply(u, *attend(q, *near(h), bias))

        @pl.when(has_right)
        def _():
            lse_copy(1, g).start()

        return 0

    lax.fori_loop(0, ng, step_f1, 0)

    def weights_of(g):
        for u in range(QG):
            upper = to_column(lse_recv[1, g, pl.ds(u, 1), :] + for_me[pl.ds(0, 1), :], eyes[1])
            second = to_column(lse_recv[0, g, pl.ds(u, 1), :] + for_me[pl.ds(1, 1), :], eye)
            column = jnp.concatenate([upper, second], axis=0)
            l_col[g * QG + u] = jnp.broadcast_to(column, (T + HALF, D))

    def step_f0(g, _):
        @pl.when(prompt)
        def _():
            q_next(lead + nh + ng + g)

        @pl.when(has_right)
        def _():
            q_arrived(2, g)

        @pl.when(has_left)
        def _():
            arrived(lse_recv.at[0, g], lse_rs.at[0, g])
            arrived(lse_recv.at[1, g], lse_rs.at[1, g])
            for u in range(QG):
                arrived(l_recv.at[1, g * QG + u], l_rs.at[1, g * QG + u])

        kv = kv_row > 0.5
        for u in range(QG):
            h = g * QG + u
            low, got = l_recv[1, h], m_recv[h]
            keys = jnp.concatenate(
                [low[:PART], got[:MID], ek[:, wide(h)], k2[:, wide(h)]], axis=0
            )
            vals = jnp.concatenate(
                [low[PART:], got[MID:], ev[:, wide(h)], v2[:, wide(h)]], axis=0
            )
            o, lse = attend(qf[pl.ds(0, HALF), wide(h)], keys, vals, bias_r[pl.ds(1, 1), :])
            lse_send[2, g, pl.ds(u, 1), :] = jnp.where(
                kv | (lane >= HALF), HIDDEN, to_row(lse, eyes[0])
            )
            rows = pl.ds(T - PART, PART)
            there = jnp.concatenate([k2[rows, wide(h)], v2[rows, wide(h)]], axis=0)
            l_send[0, h] = jnp.where(kv, there.astype(F32), o).astype(BF16)

            @pl.when(has_right)
            def _():
                l_copy(0, h).start()

        @pl.when(has_right)
        def _():
            lse_copy(2, g).start()

        @pl.when(jnp.logical_not(ends))
        def _():
            weights_of(g)

        return 0

    lax.fori_loop(0, ng, step_f0, 0)

    @pl.when(ends)
    def _():
        def step_own(g, _):
            weights_of(g)
            for u in range(QG):
                own(g * QG + u, *near(g * QG + u))
            return 0

        lax.fori_loop(0, ng, step_own, 0)

    def put(g, side, act):
        cols = pl.ds(g * OG * D, OG * D)
        to = pl.ds(pl.multiple_of(core * w + g * OG * D, D), OG * D)
        src, dst, sem = stage.at[side, :, cols], out_ref.at[:, to], oo_ss.at[side, g]

        @pl.when(core == side)
        def _():
            act(pltpu.make_async_copy(src, dst, sem), False)

        @pl.when(core != side)
        def _():
            act(remote(src, dst, sem, oo_rs.at[g], sib), True)

    def begin(cp, far):
        cp.start()

    def sent(cp, far):
        if far:
            cp.wait_send()
        else:
            cp.wait()

    def finish_heads(i, g):
        step = g * (OG // QG) + i

        @pl.when(has_left)
        def _():
            arrived(lse_recv.at[2, step], lse_rs.at[2, step])
            for u in range(QG):
                h = step * QG + u
                arrived(l_recv.at[0, h], l_rs.at[0, h])

        for u in range(QG):
            h = step * QG + u
            low, mid = l_recv[0, h], l_recv[1, h]
            keys = jnp.concatenate([low[:PART], mid[:PART]], axis=0)
            vals = jnp.concatenate([low[PART:], mid[PART:]], axis=0)
            theirs = jnp.concatenate([low, mid, m_recv[h], jnp.zeros((T - G, D), BF16)], axis=0)
            lower = to_column(
                lse_recv[2, step, pl.ds(u, 1), :] + for_me[pl.ds(0, 1), :], eyes[0]
            )
            there = jnp.concatenate([jnp.broadcast_to(lower, (HALF, D)), l_col[h]], axis=0)
            here = s_loc[h]
            s = scores(q2[:, wide(h)], keys, bias_a[...]) * C2
            top = jnp.maximum(jnp.max(s, axis=1, keepdims=True), there)
            top = jnp.maximum(here, top)
            p = jnp.exp2(s - top[:, :HALF])
            fade = jnp.exp2(here - top)
            extra = jnp.exp2(there - top)
            total = fade + extra + jnp.sum(p, axis=1, keepdims=True)
            out = o_loc[h] * fade + weigh(p, vals) + theirs.astype(F32) * extra
            out = (out / total).astype(BF16)
            lse = (top + jnp.log2(total)) * LN2
            for side in range(2):
                rows = slice(side * T, side * T + T)
                stage[side, :, wide(h)] = out[rows]
                sums[side, pl.ds(h, 1), :] = to_row(lse[rows], eye)
        return g

    def drained():
        id_sib.wait_send()
        for cp in sib_sends:
            cp.wait_send()

        @pl.when(has_right)
        def _():
            for cp in id_right:
                cp.wait_send()

            @pl.when(core == 1)
            def _():
                for cp in e_copies():
                    cp.wait_send()

            def drain(h, _):
                m_copy(h).wait_send()
                l_copy(1, h).wait_send()
                l_copy(0, h).wait_send()
                return 0

            lax.fori_loop(0, nh, drain, 0)
            for i in range(3):
                for g in range(ng):
                    lse_copy(i, g).wait_send()

        @pl.when(has_left)
        def _():
            for q in q_order:
                q_copy(*q).wait_send()

    for g in range(no):
        lax.fori_loop(0, OG // QG, finish_heads, g)
        put(g, 0, begin)
        put(g, 1, begin)

    own_sum = pltpu.make_async_copy(sums.at[core], sum_ref.at[core], sum_ss.at[0])
    far_sum = remote(sums.at[other], sum_ref.at[core], sum_ss.at[1], sum_rs, sib)
    own_sum.start()
    far_sum.start()
    drained()

    for g in range(no):
        put(g, 0, sent)
        put(g, 1, sent)
        to = pl.ds(pl.multiple_of(other * w + g * OG * D, D), OG * D)
        arrived(out_ref.at[:, to], oo_rs.at[g])
    own_sum.wait()
    far_sum.wait_send()
    arrived(sum_ref.at[other], sum_rs)


CHUNKS = 4


def finish(nh, out_in, sum_in, out_ref, sum_ref, hold, sem):
    size = out_in.shape[0] // CHUNKS
    cps = [
        pltpu.make_async_copy(
            out_in.at[pl.ds(i * size, size), :], out_ref.at[pl.ds(i * size, size), :], sem.at[i]
        )
        for i in range(CHUNKS)
    ]
    cps.append(pltpu.make_async_copy(hold, sum_ref, sem.at[CHUNKS]))
    for cp in cps[:-1]:
        cp.start()
    for i in range(2):
        hold[pl.ds(i * nh, nh), :] = sum_in[i, pl.ds(0, nh), :]
    cps[-1].start()
    for cp in cps:
        cp.wait()


def shards(mesh, queries, keys, values, segment_ids):
    n, ncp = mesh.size, mesh.shape["cp"]
    width = queries.shape[1]
    heads = width // D
    nh = heads // 2
    ng, no = nh // QG, nh // OG
    w = nh * D
    pad = -(-nh // 8) * 8
    dma = pltpu.SemaphoreType.DMA
    scratch = [
        pltpu.VMEM((4, 1, T), jnp.int32),
        pltpu.VMEM((2 * T, w), BF16),
        pltpu.VMEM((2 * T, w), BF16),
        pltpu.VMEM((2 * T, w), BF16),
        pltpu.VMEM((G, w), BF16),
        pltpu.VMEM((T, w), BF16),
        pltpu.VMEM((END, w), BF16),
        pltpu.VMEM((END, w), BF16),
        pltpu.VMEM((nh, G, D), BF16),
        pltpu.VMEM((nh, G, D), BF16),
        pltpu.VMEM((2, nh, HALF, D), BF16),
        pltpu.VMEM((2, nh, HALF, D), BF16),
        pltpu.VMEM((3, ng, 8, T), F32),
        pltpu.VMEM((3, ng, 8, T), F32),
        pltpu.VMEM((8, 3 * T), F32),
        pltpu.VMEM((2 * T, 3 * T), F32),
        pltpu.VMEM((2 * T, HALF), F32),
        pltpu.VMEM((8, T), F32),
        pltpu.VMEM((nh, T + HALF, D), F32),
        pltpu.VMEM((nh, 2 * T, D), F32),
        pltpu.VMEM((nh, 2 * T, D), F32),
        pltpu.VMEM((2, T, w), BF16),
        pltpu.VMEM((2, pad, T), F32),
        pltpu.SemaphoreType.REGULAR,
        dma((3,)),
        dma((4,)),
        dma((4,)),
        dma((3,)),
        dma((3,)),
        dma((2, 2)),
        dma((2,)),
        dma((3, nh)),
        dma((3, nh)),
        dma((nh,)),
        dma((nh,)),
        dma((2, nh)),
        dma((2, nh)),
        dma((3, ng)),
        dma((3, ng)),
        dma((2, no)),
        dma((no,)),
        dma((2,)),
        dma,
    ]
    anywhere = pl.BlockSpec(memory_space=pl.ANY)
    vmem = pl.BlockSpec(memory_space=pltpu.VMEM)
    operands = (queries, keys, values, segment_ids.reshape(1, T))
    out, sums = pl.pallas_call(
        functools.partial(kernel, n, ncp, nh),
        out_shape=(
            jax.ShapeDtypeStruct((T, width), BF16),
            jax.ShapeDtypeStruct((2, pad, T), F32),
        ),
        in_specs=[anywhere, anywhere, anywhere, anywhere],
        out_specs=(anywhere, anywhere),
        scratch_shapes=scratch,
        compiler_params=pltpu.CompilerParams(
            collective_id=0, has_side_effects=True, vmem_limit_bytes=48 * 2**20
        ),
        cost_estimate=pl.CostEstimate(
            flops=heads * T * T * D * 20, bytes_accessed=8 * T * width, transcendentals=0
        ),
    )(*[pltpu.with_memory_space_constraint(a, pltpu.HBM) for a in operands])
    return pl.pallas_call(
        functools.partial(finish, nh),
        out_shape=(
            jax.ShapeDtypeStruct((T, width), BF16),
            jax.ShapeDtypeStruct((heads, T), F32),
        ),
        in_specs=[anywhere, vmem],
        out_specs=(anywhere, anywhere),
        scratch_shapes=[pltpu.VMEM((heads, T), F32), dma((CHUNKS + 1,))],
        compiler_params=pltpu.CompilerParams(vmem_limit_bytes=48 * 2**20),
    )(out, sums)


def solution(mesh):
    both = ("grp", "cp")
    return jax.shard_map(
        functools.partial(shards, mesh),
        mesh=mesh,
        in_specs=(P(both, None), P(both, None), P(both, None), P(both)),
        out_specs=(P(both, None), P(None, both)),
        check_vma=False,
    )
```

```python
import functools
import math

import jax
import jax.numpy as jnp
from jax import lax
from jax.experimental import pallas as pl
from jax.experimental.pallas import tpu as pltpu
from jax.sharding import PartitionSpec as P

T = 128
HALF = T // 2
PART = T // 4
G = 96
MID = G // 2
END = T - PART - MID
D = 128
HIDDEN = -1e30
C2 = 1.0 / math.sqrt(D) / math.log(2.0)
LN2 = math.log(2.0)
MESH = pl.DeviceIdType.MESH
F32 = jnp.float32
BF16 = jnp.bfloat16

QG = 2
OG = 2
LINE = 16
AHEAD = 6
TWO = 2
PUMP = 18
MORE = 2
LINE = 16


def wide(h):
    return pl.ds(pl.multiple_of(h * D, D), D)


def scores(q, k, bias):
    return lax.dot_general(q, k, (((1,), (1,)), ((), ())), preferred_element_type=F32) + bias


def weigh(p, v):
    return lax.dot_general(
        p.astype(BF16), v, (((1,), (0,)), ((), ())), preferred_element_type=F32
    )


def attend(q, k, v, bias):
    s = scores(q, k, bias)
    top = jnp.max(s, axis=1, keepdims=True)
    p = jnp.exp2((s - top) * C2)
    total = jnp.sum(p, axis=1, keepdims=True)
    return weigh(p, v) * (1.0 / total), top * C2 + jnp.log2(total)


def kernel(
    n,
    ncp,
    nh,
    q_ref,
    k_ref,
    v_ref,
    id_ref,
    out_ref,
    sum_ref,
    ids,
    q2,
    k2,
    v2,
    qg,
    qf,
    ek,
    ev,
    m_send,
    m_recv,
    l_send,
    l_recv,
    lse_send,
    lse_recv,
    bias_r,
    bias_o,
    bias_a,
    for_me,
    l_col,
    o_loc,
    s_loc,
    stage,
    sums,
    go,
    id_ss,
    id_rs,
    lo_s,
    sib_ss,
    sib_rs,
    e_ss,
    e_rs,
    q_ss,
    q_rs,
    m_ss,
    m_rs,
    l_ss,
    l_rs,
    lse_ss,
    lse_rs,
    oo_ss,
    oo_rs,
    sum_ss,
    sum_rs,
):
    w = nh * D
    ng = nh // QG
    no = nh // OG
    me = lax.axis_index("grp") * ncp + lax.axis_index("cp")
    core = lax.rem(me, 2)
    first = me - core
    other = 1 - core
    has_left = first > 0
    has_right = first < n - 2
    waits = lax.rem(first, LINE) == 0
    prompt = jnp.logical_not(waits)
    ends = lax.rem(first, LINE) == LINE - 2
    lead = jnp.where(ends, PUMP, jnp.where(waits, TWO, AHEAD))

    def at(i):
        i = lax.rem(i + n, n)
        return (i // ncp, lax.rem(i, ncp))

    sib = at(first + other)
    right = [at(first + 2), at(first + 3)]
    left = [at(first - 2), at(first - 1)]
    ahead = at(me + 2)
    behind_me = at(me - 2)

    def remote(src, dst, ss, rs, to):
        return pltpu.make_async_remote_copy(
            src_ref=src, dst_ref=dst, send_sem=ss, recv_sem=rs, device_id=to, device_id_type=MESH
        )

    def greet(sem, to):
        pl.semaphore_signal(sem, inc=1, device_id=to, device_id_type=MESH)

    def arrived(dst, rs):
        remote(dst, dst, sum_ss.at[0], rs, sib).wait_recv()

    barrier = pltpu.get_barrier_semaphore()
    greet(barrier, sib)

    @pl.when(has_left)
    def _():
        greet(barrier, left[0])
        greet(barrier, left[1])

    mine = pl.ds(pl.multiple_of(core * w, D), w)
    its = pl.ds(pl.multiple_of(other * w, D), w)
    my_rows = pl.ds(pl.multiple_of(core * T, T), T)
    its_rows = pl.ds(pl.multiple_of(other * T, T), T)
    trio = ((k_ref, k2), (v_ref, v2), (q_ref, q2))
    local = [
        pltpu.make_async_copy(a.at[:, mine], b.at[my_rows, :], lo_s.at[i])
        for i, (a, b) in enumerate(trio)
    ]
    local.append(pltpu.make_async_copy(id_ref, ids.at[2 + core], lo_s.at[3]))
    for cp in local:
        cp.start()
    pl.semaphore_wait(barrier, 1 + 2 * has_right.astype(jnp.int32))

    @pl.when(has_right)
    def _():
        greet(go, right[0])
        greet(go, right[1])

    id_sib = remote(id_ref, ids.at[2 + core], id_ss.at[0], id_rs.at[2 + core], sib)
    id_right = [
        remote(id_ref, ids.at[core], id_ss.at[1 + i], id_rs.at[core], right[i]) for i in range(2)
    ]
    sib_sends = [
        remote(a.at[:, its], b.at[my_rows, :], sib_ss.at[i], sib_rs.at[i], sib)
        for i, (a, b) in enumerate(trio)
    ]

    def e_copies():
        return [
            remote(
                a.at[pl.ds(T - END, END), pl.ds(kk * w, w)],
                b,
                e_ss.at[kk, i],
                e_rs.at[i],
                right[kk],
            )
            for kk in range(2)
            for i, (a, b) in enumerate(((k_ref, ek), (v_ref, ev)))
        ]

    def q_cols(g):
        return pl.ds(pl.multiple_of(g * QG * D, D), QG * D)

    pieces = ((T, qg, 0, G), (HALF, qf, HALF, HALF), (0, qf, 0, HALF))

    def q_cut(piece, g):
        return wide(g) if piece == 0 else q_cols(g)

    def q_copy(piece, g):
        start, to, row, size = pieces[piece]
        return remote(
            q2.at[pl.ds(start, size), q_cut(piece, g)],
            to.at[pl.ds(row, size), q_cut(piece, g)],
            q_ss.at[piece, g],
            q_rs.at[piece, g],
            behind_me,
        )

    def q_arrived(piece, g):
        _, to, row, size = pieces[piece]
        arrived(to.at[pl.ds(row, size), q_cut(piece, g)], q_rs.at[piece, g])

    q_order = [(0, h) for h in range(nh)] + [(p, g) for p in (1, 2) for g in range(ng)]

    def q_next(i):
        for piece, start, count in ((0, 0, nh), (1, nh, ng), (2, nh + ng, ng)):

            @pl.when(has_left & (i >= start) & (i < start + count))
            def _():
                q_copy(piece, i - start).start()

    sib_sends[2].start()
    id_sib.start()
    sib_sends[0].start()
    sib_sends[1].start()

    @pl.when(has_right)
    def _():
        id_right[0].start()
        id_right[1].start()

        @pl.when(core == 1)
        def _():
            for cp in e_copies():
                cp.start()

    @pl.when(jnp.logical_not(has_left))
    def _():
        ids[0] = jnp.full((1, T), -1, jnp.int32)
        ids[1] = jnp.full((1, T), -1, jnp.int32)
        ek[...] = jnp.zeros(ek.shape, BF16)
        ev[...] = jnp.zeros(ev.shape, BF16)
        m_recv[...] = jnp.zeros(m_recv.shape, BF16)
        l_recv[...] = jnp.zeros(l_recv.shape, BF16)
        lse_recv[...] = jnp.full(lse_recv.shape, HIDDEN, F32)

    def iota(shape, axis):
        return lax.broadcasted_iota(jnp.int32, shape, axis)

    eye = iota((T, T), 0) == iota((T, T), 1)
    eyes = [iota((HALF, T), 0) + HALF * i == iota((HALF, T), 1) for i in range(2)]
    eye_g = iota((G, T), 0) == iota((G, T), 1)

    def to_column(r, like):
        return jnp.sum(
            jnp.where(like, jnp.broadcast_to(r, like.shape), 0.0), axis=1, keepdims=True
        )

    def to_row(x, like):
        return jnp.sum(jnp.where(like, x, 0.0), axis=0, keepdims=True)

    def bias_of(q_col, k_row):
        return jnp.where(q_col == k_row, 0.0, HIDDEN)

    def have(i):
        local[i].wait()
        arrived(trio[i][1].at[its_rows, :], sib_rs.at[i])

    have(0)
    have(1)

    have(2)
    arrived(ids.at[2 + other], id_rs.at[2 + other])
    local[3].wait()
    own = [ids[2].astype(F32), ids[3].astype(F32)]
    own_col = [to_column(r, eye) for r in own]
    for i in range(2):
        for j in range(2):
            bias_o[pl.ds(i * T, T), pl.ds((j + 1) * T, T)] = (
                bias_of(own_col[i], own[j]) if j <= i else jnp.full((T, T), HIDDEN, F32)
            )

    lane = iota((1, T), 1)

    def short(a, b):
        edge = jnp.sum(jnp.where(lane == T - PART - 1, a, 0.0), axis=1, keepdims=True)
        return edge != jnp.max(b, axis=1, keepdims=True)

    kv_row = jnp.broadcast_to(jnp.where(short(*own), 1.0, 0.0), (1, D))

    @pl.when(has_left)
    def _():
        pl.semaphore_wait(go, 2)
        for i in range(PUMP):

            @pl.when(i < lead)
            def _():
                q_copy(*q_order[i]).start()

    across = jnp.max(own[1], axis=1, keepdims=True)

    def bias_across(k_row):
        return jnp.where(k_row == across, 0.0, HIDDEN)

    for j in range(2):
        for i in range(2):
            bias_r[pl.ds(i, 1), pl.ds((j + 1) * T, T)] = bias_across(own[j])

    def m_copy(h):
        return remote(m_send.at[h], m_recv.at[h], m_ss.at[h], m_rs.at[h], ahead)

    def l_copy(part, h):
        return remote(
            l_send.at[part, h], l_recv.at[part, h], l_ss.at[part, h], l_rs.at[part, h], ahead
        )

    def lse_copy(i, g):
        return remote(
            lse_send.at[i, g], lse_recv.at[i, g], lse_ss.at[i, g], lse_rs.at[i, g], ahead
        )

    def step_g(h, _):
        q_next(lead + h)

        @pl.when(has_right)
        def _():
            q_arrived(0, h)

        kv = kv_row > 0.5
        g, u = h // QG, lax.rem(h, QG)
        o, lse = attend(
            qg[:, wide(h)], k2[:, wide(h)], v2[:, wide(h)], bias_r[pl.ds(0, 1), pl.ds(T, 2 * T)]
        )
        lse_send[0, g, pl.ds(u, 1), :] = jnp.where(kv | (lane >= G), HIDDEN, to_row(lse, eye_g))
        rows = pl.ds(T + PART, MID)
        there = jnp.concatenate([k2[rows, wide(h)], v2[rows, wide(h)]], axis=0)
        m_send[h] = jnp.where(kv, there.astype(F32), o).astype(BF16)

        @pl.when(has_right)
        def _():
            m_copy(h).start()

            @pl.when(u == QG - 1)
            def _():
                lse_copy(0, g).start()

        return 0

    lax.fori_loop(0, nh, step_g, 0, unroll=2)

    @pl.when(waits & has_left)
    def _():
        for i in range(TWO + nh, PUMP):
            q_copy(*q_order[i]).start()

    @pl.when(has_left)
    def _():
        arrived(ids.at[0], id_rs.at[0])
        arrived(ids.at[1], id_rs.at[1])
        arrived(ek, e_rs.at[0])
        arrived(ev, e_rs.at[1])

    before = [ids[i].astype(F32) for i in range(2)]
    seen = [jnp.where(short(*before), r, -1.0) for r in before]
    behind = seen[1]
    low_keys = jnp.concatenate([seen[0][:, T - PART :], behind[:, :PART]], axis=1)
    for i in range(2):
        rows = pl.ds(i * T, T)
        bias_o[rows, pl.ds(0, T)] = jnp.where(
            iota((T, T), 1) < PART, HIDDEN, bias_of(own_col[i], behind)
        )
        bias_a[rows, :] = bias_of(own_col[i], low_keys)
    bias_r[pl.ds(0, 1), pl.ds(0, T)] = jnp.where(lane < PART, HIDDEN, bias_across(behind))
    bias_r[pl.ds(1, 1), pl.ds(0, T)] = bias_across(behind)
    from_left = jnp.max(before[1], axis=1, keepdims=True)
    for i in range(2):
        for_me[pl.ds(i, 1), :] = jnp.where(own[i] == from_left, 0.0, 2.0 * HIDDEN)

    def near(h):
        none = jnp.zeros((PART, D), BF16)
        got = m_recv[h]
        keys = jnp.concatenate([none, got[:MID], ek[:, wide(h)], k2[:, wide(h)]], axis=0)
        vals = jnp.concatenate([none, got[MID:], ev[:, wide(h)], v2[:, wide(h)]], axis=0)
        return keys, vals

    def own(h, keys, vals):
        o_loc[h], lse = attend(q2[:, wide(h)], keys, vals, bias_o[...])
        s_loc[h] = jnp.broadcast_to(lse, (2 * T, D))

    def step_f1(g, _):
        @pl.when(waits)
        def _():
            for i in range(MORE):
                q_next(PUMP + g * MORE + i)

        @pl.when(prompt)
        def _():
            q_next(lead + nh + g)

        @pl.when(has_right)
        def _():
            q_arrived(1, g)

        @pl.when(has_left)
        def _():
            for u in range(QG):
                arrived(m_recv.at[g * QG + u], m_rs.at[g * QG + u])

        def reply(u, o, lse):
            h = g * QG + u
            kv = kv_row > 0.5
            lse_send[1, g, pl.ds(u, 1), :] = jnp.where(
                kv | (lane < HALF), HIDDEN, to_row(lse, eyes[1])
            )
            rows = pl.ds(T, PART)
            there = jnp.concatenate([k2[rows, wide(h)], v2[rows, wide(h)]], axis=0)
            l_send[1, h] = jnp.where(kv, there.astype(F32), o).astype(BF16)

            @pl.when(has_right)
            def _():
                l_copy(1, h).start()

        @pl.when(jnp.logical_not(ends))
        def _():
            for u in range(QG):
                h = g * QG + u
                q = jnp.concatenate([qf[pl.ds(HALF, HALF), wide(h)], q2[:, wide(h)]], axis=0)
                bias = jnp.concatenate(
                    [jnp.broadcast_to(bias_r[pl.ds(0, 1), :], (HALF, 3 * T)), bias_o[...]], axis=0
                )
                o, lse = attend(q, *near(h), bias)
                reply(u, o[:HALF], lse[:HALF])
                o_loc[h] = o[HALF:]
                s_loc[h] = jnp.broadcast_to(lse[HALF:], (2 * T, D))

        @pl.when(ends)
        def _():
            for u in range(QG):
                h = g * QG + u
                q, bias = qf[pl.ds(HALF, HALF), wide(h)], bias_r[pl.ds(0, 1), :]
                reply(u, *attend(q, *near(h), bias))

        @pl.when(has_right)
        def _():
            lse_copy(1, g).start()

        return 0

    lax.fori_loop(0, ng, step_f1, 0)

    def weights_of(g):
        for u in range(QG):
            upper = to_column(lse_recv[1, g, pl.ds(u, 1), :] + for_me[pl.ds(0, 1), :], eyes[1])
            second = to_column(lse_recv[0, g, pl.ds(u, 1), :] + for_me[pl.ds(1, 1), :], eye)
            column = jnp.concatenate([upper, second], axis=0)
            l_col[g * QG + u] = jnp.broadcast_to(column, (T + HALF, D))

    def step_f0(g, _):
        @pl.when(prompt)
        def _():
            q_next(lead + nh + ng + g)

        @pl.when(has_right)
        def _():
            q_arrived(2, g)

        @pl.when(has_left)
        def _():
            arrived(lse_recv.at[0, g], lse_rs.at[0, g])
            arrived(lse_recv.at[1, g], lse_rs.at[1, g])
            for u in range(QG):
                arrived(l_recv.at[1, g * QG + u], l_rs.at[1, g * QG + u])

        kv = kv_row > 0.5
        for u in range(QG):
            h = g * QG + u
            low, got = l_recv[1, h], m_recv[h]
            keys = jnp.concatenate(
                [low[:PART], got[:MID], ek[:, wide(h)], k2[:, wide(h)]], axis=0
            )
            vals = jnp.concatenate(
                [low[PART:], got[MID:], ev[:, wide(h)], v2[:, wide(h)]], axis=0
            )
            o, lse = attend(qf[pl.ds(0, HALF), wide(h)], keys, vals, bias_r[pl.ds(1, 1), :])
            lse_send[2, g, pl.ds(u, 1), :] = jnp.where(
                kv | (lane >= HALF), HIDDEN, to_row(lse, eyes[0])
            )
            rows = pl.ds(T - PART, PART)
            there = jnp.concatenate([k2[rows, wide(h)], v2[rows, wide(h)]], axis=0)
            l_send[0, h] = jnp.where(kv, there.astype(F32), o).astype(BF16)

            @pl.when(has_right)
            def _():
                l_copy(0, h).start()

        @pl.when(has_right)
        def _():
            lse_copy(2, g).start()

        @pl.when(jnp.logical_not(ends))
        def _():
            weights_of(g)

        return 0

    lax.fori_loop(0, ng, step_f0, 0, unroll=2)

    @pl.when(ends)
    def _():
        def step_own(g, _):
            weights_of(g)
            for u in range(QG):
                own(g * QG + u, *near(g * QG + u))
            return 0

        lax.fori_loop(0, ng, step_own, 0)

    def put(g, side, act):
        cols = pl.ds(g * OG * D, OG * D)
        to = pl.ds(pl.multiple_of(core * w + g * OG * D, D), OG * D)
        src, dst, sem = stage.at[side, :, cols], out_ref.at[:, to], oo_ss.at[side, g]

        @pl.when(core == side)
        def _():
            act(pltpu.make_async_copy(src, dst, sem), False)

        @pl.when(core != side)
        def _():
            act(remote(src, dst, sem, oo_rs.at[g], sib), True)

    def begin(cp, far):
        cp.start()

    def sent(cp, far):
        if far:
            cp.wait_send()
        else:
            cp.wait()

    def finish_heads(i, g):
        step = g * (OG // QG) + i

        @pl.when(has_left)
        def _():
            arrived(lse_recv.at[2, step], lse_rs.at[2, step])
            for u in range(QG):
                h = step * QG + u
                arrived(l_recv.at[0, h], l_rs.at[0, h])

        for u in range(QG):
            h = step * QG + u
            low, mid = l_recv[0, h], l_recv[1, h]
            keys = jnp.concatenate([low[:PART], mid[:PART]], axis=0)
            vals = jnp.concatenate([low[PART:], mid[PART:]], axis=0)
            theirs = jnp.concatenate([low, mid, m_recv[h], jnp.zeros((T - G, D), BF16)], axis=0)
            lower = to_column(
                lse_recv[2, step, pl.ds(u, 1), :] + for_me[pl.ds(0, 1), :], eyes[0]
            )
            there = jnp.concatenate([jnp.broadcast_to(lower, (HALF, D)), l_col[h]], axis=0)
            here = s_loc[h]
            s = scores(q2[:, wide(h)], keys, bias_a[...]) * C2
            top = jnp.maximum(jnp.max(s, axis=1, keepdims=True), there)
            top = jnp.maximum(here, top)
            p = jnp.exp2(s - top[:, :HALF])
            fade = jnp.exp2(here - top)
            extra = jnp.exp2(there - top)
            total = fade + extra + jnp.sum(p, axis=1, keepdims=True)
            out = o_loc[h] * fade + weigh(p, vals) + theirs.astype(F32) * extra
            out = (out / total).astype(BF16)
            lse = (top + jnp.log2(total)) * LN2
            for side in range(2):
                rows = slice(side * T, side * T + T)
                stage[side, :, wide(h)] = out[rows]
                sums[side, pl.ds(h, 1), :] = to_row(lse[rows], eye)
        return g

    def drained():
        id_sib.wait_send()
        for cp in sib_sends:
            cp.wait_send()

        @pl.when(has_right)
        def _():
            for cp in id_right:
                cp.wait_send()

            @pl.when(core == 1)
            def _():
                for cp in e_copies():
                    cp.wait_send()

            def drain(h, _):
                m_copy(h).wait_send()
                l_copy(1, h).wait_send()
                l_copy(0, h).wait_send()
                return 0

            lax.fori_loop(0, nh, drain, 0)
            for i in range(3):
                for g in range(ng):
                    lse_copy(i, g).wait_send()

        @pl.when(has_left)
        def _():
            for q in q_order:
                q_copy(*q).wait_send()

    for g in range(no):
        lax.fori_loop(0, OG // QG, finish_heads, g)
        put(g, 0, begin)
        put(g, 1, begin)

    own_sum = pltpu.make_async_copy(sums.at[core], sum_ref.at[core], sum_ss.at[0])
    far_sum = remote(sums.at[other], sum_ref.at[core], sum_ss.at[1], sum_rs, sib)
    own_sum.start()
    far_sum.start()
    drained()

    for g in range(no):
        put(g, 0, sent)
        put(g, 1, sent)
        to = pl.ds(pl.multiple_of(other * w + g * OG * D, D), OG * D)
        arrived(out_ref.at[:, to], oo_rs.at[g])
    own_sum.wait()
    far_sum.wait_send()
    arrived(sum_ref.at[other], sum_rs)


CHUNKS = 4


def finish(nh, out_in, sum_in, out_ref, sum_ref, hold, sem):
    size = out_in.shape[0] // CHUNKS
    cps = [
        pltpu.make_async_copy(
            out_in.at[pl.ds(i * size, size), :], out_ref.at[pl.ds(i * size, size), :], sem.at[i]
        )
        for i in range(CHUNKS)
    ]
    cps.append(pltpu.make_async_copy(hold, sum_ref, sem.at[CHUNKS]))
    for cp in cps[:-1]:
        cp.start()
    for i in range(2):
        hold[pl.ds(i * nh, nh), :] = sum_in[i, pl.ds(0, nh), :]
    cps[-1].start()
    for cp in cps:
        cp.wait()


def shards(mesh, queries, keys, values, segment_ids):
    n, ncp = mesh.size, mesh.shape["cp"]
    width = queries.shape[1]
    heads = width // D
    nh = heads // 2
    ng, no = nh // QG, nh // OG
    w = nh * D
    pad = -(-nh // 8) * 8
    dma = pltpu.SemaphoreType.DMA
    scratch = [
        pltpu.VMEM((4, 1, T), jnp.int32),
        pltpu.VMEM((2 * T, w), BF16),
        pltpu.VMEM((2 * T, w), BF16),
        pltpu.VMEM((2 * T, w), BF16),
        pltpu.VMEM((G, w), BF16),
        pltpu.VMEM((T, w), BF16),
        pltpu.VMEM((END, w), BF16),
        pltpu.VMEM((END, w), BF16),
        pltpu.VMEM((nh, G, D), BF16),
        pltpu.VMEM((nh, G, D), BF16),
        pltpu.VMEM((2, nh, HALF, D), BF16),
        pltpu.VMEM((2, nh, HALF, D), BF16),
        pltpu.VMEM((3, ng, 8, T), F32),
        pltpu.VMEM((3, ng, 8, T), F32),
        pltpu.VMEM((8, 3 * T), F32),
        pltpu.VMEM((2 * T, 3 * T), F32),
        pltpu.VMEM((2 * T, HALF), F32),
        pltpu.VMEM((8, T), F32),
        pltpu.VMEM((nh, T + HALF, D), F32),
        pltpu.VMEM((nh, 2 * T, D), F32),
        pltpu.VMEM((nh, 2 * T, D), F32),
        pltpu.VMEM((2, T, w), BF16),
        pltpu.VMEM((2, pad, T), F32),
        pltpu.SemaphoreType.REGULAR,
        dma((3,)),
        dma((4,)),
        dma((4,)),
        dma((3,)),
        dma((3,)),
        dma((2, 2)),
        dma((2,)),
        dma((3, nh)),
        dma((3, nh)),
        dma((nh,)),
        dma((nh,)),
        dma((2, nh)),
        dma((2, nh)),
        dma((3, ng)),
        dma((3, ng)),
        dma((2, no)),
        dma((no,)),
        dma((2,)),
        dma,
    ]
    anywhere = pl.BlockSpec(memory_space=pl.ANY)
    vmem = pl.BlockSpec(memory_space=pltpu.VMEM)
    operands = (queries, keys, values, segment_ids.reshape(1, T))
    out, sums = pl.pallas_call(
        functools.partial(kernel, n, ncp, nh),
        out_shape=(
            jax.ShapeDtypeStruct((T, width), BF16),
            jax.ShapeDtypeStruct((2, pad, T), F32),
        ),
        in_specs=[anywhere, anywhere, anywhere, anywhere],
        out_specs=(anywhere, anywhere),
        scratch_shapes=scratch,
        compiler_params=pltpu.CompilerParams(
            collective_id=0, has_side_effects=True, vmem_limit_bytes=48 * 2**20
        ),
        cost_estimate=pl.CostEstimate(
            flops=heads * T * T * D * 20, bytes_accessed=8 * T * width, transcendentals=0
        ),
    )(*[pltpu.with_memory_space_constraint(a, pltpu.HBM) for a in operands])
    return pl.pallas_call(
        functools.partial(finish, nh),
        out_shape=(
            jax.ShapeDtypeStruct((T, width), BF16),
            jax.ShapeDtypeStruct((heads, T), F32),
        ),
        in_specs=[anywhere, vmem],
        out_specs=(anywhere, anywhere),
        scratch_shapes=[pltpu.VMEM((heads, T), F32), dma((CHUNKS + 1,))],
        compiler_params=pltpu.CompilerParams(vmem_limit_bytes=48 * 2**20),
    )(out, sums)


def solution(mesh):
    both = ("grp", "cp")
    return jax.shard_map(
        functools.partial(shards, mesh),
        mesh=mesh,
        in_specs=(P(both, None), P(both, None), P(both, None), P(both)),
        out_specs=(P(both, None), P(None, both)),
        check_vma=False,
    )
```
